512 devices in a mesh: space: 128 (over y, z, core), scene: 4 (over x).
Axes of the slice: x: 4, y: 8, z: 8, core: 2. Of those that a mesh axis runs over, the one named last changes fastest.
Arguments:
- coarse_features: bfloat16 [4, 8192, 128], P('scene', 'space'), may hold values from -6 to 6
- child_counts: int32 [4, 8192], P('scene', 'space'), may hold values from 4 to 8
- neighbour_rows: int32 [4, 27, 65536], P('scene', None, 'space'), may hold values from -1 to 95, as said below
- fine_owners: int32 [4, 65536, 1], P('scene', 'space'), may hold values from 0 to 127; in each aligned block of 512 rows (0 to 511, 512 to 1023, ..., all dimensions but the last counted through in order) at most 6 rows name the same one
- weights: bfloat16 [27, 128, 64], replicated, may hold values from -0.1875 to 0.1875
- cotangent: bfloat16 [4, 16384, 6, 64], P('scene', 'space'), may hold values from -0.75 to 0.75
Outputs:
- fine_out: bfloat16 [4, 16384, 6, 64], P('scene', 'space')
- coarse_grad: bfloat16 [4, 8192, 128], P('scene', 'space')
- weight_grad: float32 [27, 128, 64], replicated
The draws below stay inside these ranges and needn't reach their ends.
Inputs may be any that keep to these rules, and one draw needn't show every extreme that they name: `neighbour_rows`: A valid row is 16 + c + d for the slot's coarse row c and some d with |d| <= 16; the last slot of a slab names row 95 at offset 0 and the first names row 0 at offset 1. `fine_owners`: within the slots of one device, at most 6 name the same owner, a bound that some block reaches.
All inputs are finite; a program needn't handle non-finite values.
Results may differ from the reference program's by a relative error of at most 0.00105.
Values may be sent and summed in bfloat16 or wider, within the bound.
A program may use at most 64 MiB of HBM per device.

```python
import math
import jax
import jax.numpy as jnp
import numpy as np
from jax import lax

CIN = 128
COUT = 64
KVOL = 27
F_DEV = 512
C_DEV = 64
HALO = 16
CAP = 6
COARSE = 8192
FINE = 65536
N_SPACE = 128
N_SCENE = 4


def draw_neighbour_rows(key, part):
    key_delta, key_keep = jax.random.split(jax.random.fold_in(key, 11))
    shape = (N_SCENE, KVOL, FINE)
    slot = jnp.arange(FINE, dtype=jnp.int32) % F_DEV
    parent = (slot // 8)[None, None, :]
    delta = jax.random.randint(key_delta, shape, -HALO, HALO + 1, dtype=jnp.int32)
    keep = jax.random.randint(key_keep, shape, 0, 4, dtype=jnp.int32) == 0
    found = jnp.where(keep, HALO + parent + delta, -1)
    offset = jnp.arange(KVOL, dtype=jnp.int32)[None, :, None]
    last = (slot == F_DEV - 1)[None, None, :]
    first = (slot == 0)[None, None, :]
    found = jnp.where(last & (offset == 0), C_DEV + 2 * HALO - 1, found)
    found = jnp.where(first & (offset == 1), 0, found)
    return found.astype(jnp.int32)


def touch_ends(array, key, smallest, top_value):
    longest = array.shape.index(max(array.shape))
    spots = []
    for shift in (0, 1):
        where = [jax.random.randint(jax.random.fold_in(key, axis), (), 0, length) for axis, length in enumerate(array.shape)]
        where[longest] = (where[longest] + shift) % array.shape[longest]
        spots.append(tuple(where))
    return array.at[spots[0]].set(smallest).at[spots[1]].set(top_value)


def steps_of(key, shape, pieces, least, high):
    def one(position, blocks):
        steps = jax.random.uniform(jax.random.fold_in(jax.random.fold_in(key, 6), position), (blocks,), jnp.float32, least / len(pieces), high / len(pieces))
        return jnp.repeat(jnp.exp(steps), shape[position] // blocks).reshape((-1,) + (1,) * (len(shape) - position - 1))

    factor_of = one(*pieces[0])
    for cut in pieces[1:]:
        factor_of = factor_of * one(*cut)
    return factor_of


def assign_block(key, own, number, rows, number_of, top, limit, lean):
    ranking = jax.random.permutation(key, number_of)
    packed, common = shares(number_of, rows * top, limit, lean, True), shares(number_of, rows * top, limit, lean, False)
    places = jnp.arange(number_of)

    def named(sizes, offset_by):
        used = int((sizes > 0).sum())
        fixed = max(1, used // 4)
        moved = fixed + (places - fixed + offset_by * (used - fixed)) % max(1, number_of - fixed)
        return jnp.zeros((number_of,), jnp.int32).at[ranking[jnp.where(places < fixed, places, moved)]].set(jnp.asarray(sizes, jnp.int32))

    sizes = jnp.where(number % 4 == 0, named(packed, number // 4), named(common, number - number // 4 - 1))
    mixed = jax.random.permutation(jax.random.fold_in(own, 3), number_of)
    donor, sink = mixed[0:number_of // 2 * 2:2], mixed[1:number_of // 2 * 2:2]
    margin = jnp.minimum(sizes[donor] - 1, limit - sizes[sink]) // 2
    margin = jnp.where((donor == ranking[0]) | (sink == ranking[0]) | (sizes[sink] == 0), 0, jnp.maximum(margin, 0))
    moved = jax.random.randint(jax.random.fold_in(own, 4), (number_of // 2,), 0, 1 << 20) % (margin + 1)
    sizes = sizes.at[donor].add(-moved).at[sink].add(moved)
    labels = jnp.searchsorted(jnp.cumsum(sizes), jnp.arange(rows * top), side="right").astype(jnp.int32)
    grid = labels.reshape(top, rows).T
    grid = grid[jax.random.permutation(jax.random.fold_in(own, 1), rows)]
    offset_by = jax.random.randint(jax.random.fold_in(own, 2), (rows, 1), 0, top)
    return jnp.take_along_axis(grid, (jnp.arange(top)[None, :] + offset_by) % top, axis=1)


def shares(count, total, reach, slope, full):
    weights = [(1 << 20) // math.isqrt(rank ** slope) + 1 for rank in range(1, count + 1)]
    largest = reach if full else min(reach, max(-(-total // count), total * weights[0] // sum(weights)))
    least = 1 if total - largest >= count - 1 else 0
    given, spare = [largest] + [least] * (count - 1), total - largest - least * (count - 1)
    while spare > 0:
        candidates = [i for i in range(1, count) if given[i] < largest] or [i for i in range(1, count) if given[i] < reach]
        mass, budget = sum([weights[i] for i in candidates]), spare
        for i in candidates:
            more = min(reach - given[i], max(1, budget * weights[i] // mass), spare)
            given[i] = given[i] + more
            spare = spare - more
    return np.array(given)


def scatter_about(rng, shape, scale, most, cuts=(), held_as=jnp.bfloat16):
    array = scale * jax.random.normal(rng, shape, jnp.float32)
    if cuts:
        array = array * steps_of(rng, shape, cuts, -0.22, 0.18)
    return jnp.clip(array, -most, most).astype(held_as)


def setup_inputs(seed: int = 0) -> dict:
    key_list = jax.random.split(jax.random.key(seed), 7)
    coarse_features = scatter_about(key_list[0], (N_SCENE, COARSE, CIN), 1.0, 6.0, ((0, 4), (1, 128)))
    child_counts = touch_ends(jax.random.randint(key_list[1], (N_SCENE, COARSE), 4, 9), jax.random.fold_in(key_list[1], 1), 4, 8).astype(jnp.int32)
    neighbour_rows = draw_neighbour_rows(jax.random.fold_in(key_list[6], 71), 0)
    fine_owners_keys = jax.random.split(jax.random.fold_in(key_list[3], 1), N_SCENE * FINE // F_DEV)
    fine_owners_turns = jax.random.permutation(jax.random.fold_in(key_list[3], 3), N_SCENE * FINE // F_DEV)
    fine_owners = jax.vmap(lambda own, number: assign_block(jax.random.fold_in(key_list[3], 2), own, number, F_DEV, N_SPACE, 1, CAP, 1))(fine_owners_keys, fine_owners_turns).reshape((N_SCENE, FINE, 1))
    weights = scatter_about(key_list[4], (KVOL, CIN, COUT), (7 * CIN) ** -0.5, 0.1875)
    cotangent = scatter_about(key_list[5], (N_SCENE, N_SPACE * N_SPACE, CAP, COUT), 0.125, 0.75, ((0, 4), (1, 128)))
    return dict(coarse_features=coarse_features, child_counts=child_counts, neighbour_rows=neighbour_rows, fine_owners=fine_owners, weights=weights, cotangent=cotangent)


def gather_rows(table, rows):
    found = jnp.take(table, jnp.maximum(rows, 0), axis=0)
    return jnp.where((rows >= 0)[:, None], found, jnp.zeros_like(found))


def forward_block(table, rows_all, weights):
    def step(total, item):
        rows, kernel = item
        return total + jnp.dot(gather_rows(table, rows), kernel, preferred_element_type=jnp.float32), None
    start = jnp.zeros((rows_all.shape[1], weights.shape[2]), jnp.float32)
    total, _ = lax.scan(step, start, (rows_all, weights))
    return total


def backward_block(table, rows_all, weights, slot_grad):
    def step(grad_table, item):
        rows, kernel = item
        found = gather_rows(table, rows)
        kernel_grad = jnp.dot(found.T, slot_grad, preferred_element_type=jnp.float32)
        term = jnp.dot(slot_grad, kernel.T, preferred_element_type=jnp.float32)
        term = jnp.where((rows >= 0)[:, None], term, jnp.zeros_like(term))
        grad_table = grad_table.at[jnp.maximum(rows, 0)].add(term)
        return grad_table, kernel_grad
    start = jnp.zeros((table.shape[0], weights.shape[1]), jnp.float32)
    return lax.scan(step, start, (rows_all, weights))


def slot_ranks(owners):
    onehot = (owners[:, None] == jnp.arange(N_SPACE, dtype=jnp.int32)[None, :]).astype(jnp.int32)
    return jnp.sum(jnp.cumsum(onehot, axis=0) * onehot, axis=1) - 1


def reference(coarse_features, child_counts, neighbour_rows, fine_owners, weights, cotangent):
    blocks = N_SCENE * N_SPACE
    extent = C_DEV + 2 * HALO
    feats = coarse_features.reshape(N_SCENE, N_SPACE, C_DEV, CIN)
    zero = jnp.zeros((N_SCENE, 1, HALO, CIN), coarse_features.dtype)
    lower = jnp.concatenate([zero, feats[:, :-1, C_DEV - HALO:]], axis=1)
    upper = jnp.concatenate([feats[:, 1:, :HALO], zero], axis=1)
    table = jnp.concatenate([lower, feats, upper], axis=2).reshape(blocks, extent, CIN)
    rows = neighbour_rows.reshape(N_SCENE, KVOL, N_SPACE, F_DEV).transpose(0, 2, 1, 3).reshape(blocks, KVOL, F_DEV)
    counts = child_counts.reshape(blocks, C_DEV)
    valid = (jnp.arange(8, dtype=jnp.int32)[None, None, :] < counts[:, :, None]).reshape(blocks, F_DEV)
    owners = fine_owners.reshape(blocks, F_DEV)
    totals = lax.map(lambda item: forward_block(item[0], item[1], weights), (table, rows))
    slot_out = jnp.where(valid[:, :, None], totals, jnp.zeros_like(totals)).astype(jnp.bfloat16)
    ranks = lax.map(slot_ranks, owners)
    block_index = jnp.arange(blocks, dtype=jnp.int32)
    scene_index = jnp.broadcast_to((block_index // N_SPACE)[:, None], (blocks, F_DEV))
    source = (block_index % N_SPACE)[:, None]
    dest = owners * N_SPACE + source
    fine_out = jnp.zeros((N_SCENE, N_SPACE * N_SPACE, CAP, COUT), jnp.bfloat16)
    fine_out = fine_out.at[scene_index, dest, ranks].set(slot_out)
    slot_grad = cotangent[scene_index, dest, ranks]
    slot_grad = jnp.where(valid[:, :, None], slot_grad, jnp.zeros_like(slot_grad))

    def block_step(carry, item):
        table_b, rows_b, grad_b = item
        grad_table, kernel_grads = backward_block(table_b, rows_b, weights, grad_b)
        return carry + kernel_grads, grad_table

    weight_grad, grad_tables = lax.scan(block_step, jnp.zeros((KVOL, CIN, COUT), jnp.float32), (table, rows, slot_grad))
    grad_tables = grad_tables.reshape(N_SCENE, N_SPACE, extent, CIN)
    own = grad_tables[:, :, HALO:HALO + C_DEV]
    zero_grad = jnp.zeros((N_SCENE, 1, HALO, CIN), jnp.float32)
    from_next = jnp.concatenate([grad_tables[:, 1:, :HALO], zero_grad], axis=1)
    from_prev = jnp.concatenate([zero_grad, grad_tables[:, :-1, HALO + C_DEV:]], axis=1)
    own = own.at[:, :, C_DEV - HALO:].add(from_next)
    own = own.at[:, :, :HALO].add(from_prev)
    coarse_grad = own.reshape(N_SCENE, COARSE, CIN).astype(jnp.bfloat16)
    return (fine_out, coarse_grad, weight_grad)
```

```python
import jax
import jax.numpy as jnp
from jax import lax
from jax.experimental import pallas as pl
from jax.experimental.pallas import tpu as pltpu
from jax.sharding import PartitionSpec as P

KVOL, CIN, COUT = 27, 128, 64
SLOTS, COARSE, HALO, CAP = 512, 64, 16, 6
NY, NZ, NC, NX = 8, 8, 2, 4
NJ = NZ * NC
NS = NY * NJ
TAB = 128
WIDE = CAP * COUT
ROWS = KVOL * COUT
HALF = ROWS // NC
QUART = HALF // NX
PART = 32
MESH = pl.DeviceIdType.MESH
F32, BF16 = jnp.float32, jnp.bfloat16


def dot(a, b, dims):
    return lax.dot_general(a, b, (dims, ((), ())), preferred_element_type=F32)


def nn(a, b):
    return dot(a, b, ((1,), (0,)))


def nt(a, b):
    return dot(a, b, ((1,), (1,)))


def split(value):
    high = value.astype(BF16)
    return high, (value - high.astype(F32)).astype(BF16)


def iota(shape, dim):
    return lax.broadcasted_iota(jnp.int32, shape, dim)


def kernel(
    feats, counts, rows, owners, weights, cot,
    fine, coarse, wgrad,
    table, onehot, place, wt, zz, st,
    c1, c2s, c2, f1s, f1, f2s,
    grad, rim_low, rim_high,
    w0, l1, a1, l2, a2, l3, a3, l4, b3, g3, g2,
    y_send, y_recv, j_send, j_recv, e_send, e_recv,
    z_send, z_recv, x_send, x_recv, p_send, p_recv,
):
    s, x = lax.axis_index("space"), lax.axis_index("scene")
    y, j = s // NJ, s % NJ
    z, c = j // NC, j % NC
    up, down = (s + 1) % NS, (s + NS - 1) % NS
    partner = y * NJ + z * NC + 1 - c

    def at(space, scene=None):
        return {"space": space, "scene": x if scene is None else scene}

    def y_peer(p):
        return (y + p) % NY

    def j_peer(p):
        return (j + p) % NJ

    def z_peer(p):
        return (z + p) % NZ

    def x_peer(p):
        return (x + p) % NX

    started = []

    def send(src, dst, send_sem, recv_sem, device):
        copy = pltpu.make_async_remote_copy(
            src_ref=src, dst_ref=dst, send_sem=send_sem, recv_sem=recv_sem,
            device_id=device, device_id_type=MESH,
        )
        copy.start()
        started.append(copy)
        return copy

    def over_y(n, src, dst):
        return [
            send(src(y_peer(p)), dst, y_send.at[n, p], y_recv.at[n, p], at(y_peer(p) * NJ + j))
            for p in range(1, NY)
        ]

    def over_j(n, src, dst):
        return [
            send(src(j_peer(p)), dst, j_send.at[n, p], j_recv.at[n, p], at(y * NJ + j_peer(p)))
            for p in range(1, NJ)
        ]

    def over_z(n, src, dst):
        return [
            send(src(z_peer(p)), dst, z_send.at[n, p], z_recv.at[n, p], at(y * NJ + z_peer(p) * NC + c))
            for p in range(1, NZ)
        ]

    def over_x(n, src, dst):
        return [
            send(src(x_peer(p)), dst, x_send.at[n, p], x_recv.at[n, p], at(s, x_peer(p)))
            for p in range(1, NX)
        ]

    def arrived(copies):
        for copy in copies:
            copy.wait_recv()

    barrier = pltpu.get_barrier_semaphore()
    peers = [at(y_peer(p) * NJ + j) for p in range(1, NY)]
    peers += [at(y * NJ + j_peer(p)) for p in range(1, NJ)]
    peers += [at(s, x_peer(p)) for p in range(1, NX)]
    peers += [at(up), at(down)]
    for peer in peers:
        pl.semaphore_signal(barrier, inc=1, device_id=peer, device_id_type=MESH)
    table[pl.ds(HALO, COARSE), :] = feats[...]
    table[pl.ds(HALO + COARSE + HALO, TAB - COARSE - 2 * HALO), :] = jnp.zeros(
        (TAB - COARSE - 2 * HALO, CIN), BF16
    )
    pl.semaphore_wait(barrier, len(peers))

    cot_first = over_y(0, lambda d: cot.at[d], c1.at[y])
    halo_up = send(
        feats.at[pl.ds(COARSE - HALO, HALO)], table.at[pl.ds(0, HALO)],
        e_send.at[0], e_recv.at[0], at(up),
    )
    halo_down = send(
        feats.at[pl.ds(0, HALO)], table.at[pl.ds(HALO + COARSE, HALO)],
        e_send.at[1], e_recv.at[1], at(down),
    )
    c1[y] = cot[y]

    line = iota((TAB, SLOTS), 0)
    owner_of = (line & (NY - 1)) * NJ + (line >> 3)
    named = owner_of == owners[...]
    named_bf = jnp.where(named, 1.0, 0.0).astype(BF16)
    earlier = jnp.where(iota((SLOTS, SLOTS), 0) < iota((SLOTS, SLOTS), 1), 1.0, 0.0).astype(BF16)
    before = nn(named_bf, earlier)
    for r in range(CAP):
        place[pl.ds(r * TAB, TAB), :] = jnp.where(named & (before == r), 1.0, 0.0).astype(BF16)
    spread = jnp.where(iota((COARSE, SLOTS), 0) == (iota((COARSE, SLOTS), 1) >> 3), 1.0, 0.0).astype(BF16)
    many = jnp.broadcast_to(counts[...], (8, COARSE)).astype(F32).astype(BF16)
    limit = nn(many, spread)[0:1]
    valid = (iota((1, SLOTS), 1) & 7).astype(F32) < limit
    for k in range(KVOL):
        onehot[pl.ds(k * TAB, TAB), :] = jnp.where(line == rows[pl.ds(k, 1), :], 1.0, 0.0).astype(BF16)
        wt[pl.ds(k * COUT, COUT), :] = weights[k].T

    square = (TAB, TAB)
    to_j = jnp.where(
        iota(square, 1) == (iota(square, 0) & (NY - 1)) * NJ + (iota(square, 0) >> 3), 1.0, 0.0
    ).astype(BF16)
    to_y = jnp.where(
        iota(square, 1) == (iota(square, 0) & (NJ - 1)) * NY + (iota(square, 0) >> 4), 1.0, 0.0
    ).astype(BF16)

    arrived(cot_first)
    c2s[...] = nn(to_j, c1[...].reshape(NS, WIDE)).reshape(NJ, NY, WIDE).astype(BF16)
    cot_second = over_j(0, lambda d: c2s.at[d], c2.at[j])
    c2[j] = c2s[j]

    arrived([halo_up, halo_down])

    @pl.when(s == 0)
    def _():
        table[pl.ds(0, HALO), :] = jnp.zeros((HALO, CIN), BF16)

    @pl.when(s == NS - 1)
    def _():
        table[pl.ds(HALO + COARSE, HALO), :] = jnp.zeros((HALO, CIN), BF16)

    features = table[...]
    for k in range(KVOL):
        high, low = split(nt(wt[pl.ds(k * COUT, COUT), :], features))
        zz[pl.ds(0, COUT), pl.ds(k * TAB, TAB)] = high
        zz[pl.ds(COUT, COUT), pl.ds(k * TAB, TAB)] = low
    both = nn(zz[...], onehot[...])
    slot_out = jnp.where(valid, both[:COUT] + both[COUT:], 0.0).astype(BF16)
    for r in range(CAP):
        f1s[:, :, pl.ds(r * COUT, COUT)] = (
            nt(place[pl.ds(r * TAB, TAB), :], slot_out).reshape(NJ, NY, COUT).astype(BF16)
        )
    fine_first = over_j(1, lambda d: f1s.at[d], f1.at[j])
    f1[j] = f1s[j]

    arrived(cot_second)
    turned = c2[...].astype(F32).reshape(NS, WIDE).T.astype(BF16)
    turned = jnp.concatenate([turned[r * COUT:(r + 1) * COUT] for r in range(CAP)], axis=1)
    slot_grad = jnp.where(valid, nn(turned, place[...]), 0.0).astype(BF16)
    for k in range(KVOL):
        high, low = split(nt(slot_grad, onehot[pl.ds(k * TAB, TAB), :]))
        st[pl.ds(k * COUT, COUT), pl.ds(0, TAB)] = high
        st[pl.ds(k * COUT, COUT), pl.ds(TAB, TAB)] = low
    twice = jnp.concatenate([features, features], axis=0)
    w0[1 - c] = nn(st[pl.ds(pl.multiple_of((1 - c) * HALF, 16), HALF), :], twice)
    reduce_core = send(w0.at[1 - c], l1, p_send.at[0], p_recv.at[0], at(partner))
    w0[c] = nn(st[pl.ds(pl.multiple_of(c * HALF, 16), HALF), :], twice)

    total = jnp.zeros((CIN, 2 * TAB), F32)
    for k in range(KVOL):
        total = total + nn(weights[k], st[pl.ds(k * COUT, COUT), :])
    grad[...] = (total[:, :TAB] + total[:, TAB:]).T
    rim_down = send(grad.at[pl.ds(0, HALO)], rim_high, e_send.at[2], e_recv.at[2], at(down))
    rim_up = send(
        grad.at[pl.ds(HALO + COARSE, HALO)], rim_low, e_send.at[3], e_recv.at[3], at(up)
    )

    arrived([reduce_core])
    for q in range(NX):
        a1[q] = w0[c, pl.ds(q * QUART, QUART), :] + l1[pl.ds(q * QUART, QUART), :]
    reduce_x = over_x(0, lambda d: a1.at[d], l2.at[x])

    arrived(fine_first)
    f2s[...] = (
        nn(to_y, f1[...].astype(F32).reshape(NS, WIDE).astype(BF16)).astype(BF16).reshape(NY, NJ, WIDE)
    )
    fine_second = over_y(1, lambda d: f2s.at[d], fine.at[y])
    fine[y] = f2s[y]

    a2[pl.ds(QUART, NZ * PART - QUART), :] = jnp.zeros((NZ * PART - QUART, CIN), F32)
    arrived(reduce_x)
    mine = a1[x]
    for p in range(1, NX):
        mine = mine + l2[x_peer(p)]
    a2[pl.ds(0, QUART), :] = mine

    def part(ref, d):
        return ref.at[pl.ds(pl.multiple_of(d * PART, PART), PART)]

    reduce_z = over_z(0, lambda d: part(a2, d), l3.at[z])

    arrived([rim_down, rim_up])
    own = grad[pl.ds(HALO, COARSE), :]
    low = rim_low[...] * jnp.where(s == 0, 0.0, 1.0)
    high = rim_high[...] * jnp.where(s == NS - 1, 0.0, 1.0)
    coarse[pl.ds(0, HALO), :] = (own[:HALO] + low).astype(BF16)
    coarse[pl.ds(HALO, COARSE - 2 * HALO), :] = own[HALO:COARSE - HALO].astype(BF16)
    coarse[pl.ds(COARSE - HALO, HALO), :] = (own[COARSE - HALO:] + high).astype(BF16)

    arrived(reduce_z)
    mine = part(a2, z)[...]
    for p in range(1, NZ):
        mine = mine + l3[z_peer(p)]
    a3[...] = mine
    gather_y = over_y(2, lambda d: a3, l4.at[y])
    l4[y] = mine
    arrived(gather_y)
    done = l4[0]
    for q in range(1, NY):
        done = done + l4[q]
    b3[...] = done
    gather_z = over_z(1, lambda d: b3, part(g3, z))
    part(g3, z)[...] = done
    arrived(gather_z)
    gather_x = over_x(1, lambda d: g3.at[pl.ds(0, QUART)], g2.at[x])
    g2[x] = g3[pl.ds(0, QUART), :]
    arrived(gather_x)
    gather_core = send(g2, wgrad.at[c], p_send.at[1], p_recv.at[1], at(partner))
    wgrad[c] = g2[...]
    arrived([gather_core])
    arrived(fine_second)
    for copy in started:
        copy.wait_send()


def on_device(coarse_features, child_counts, neighbour_rows, fine_owners, weights, cotangent):
    vmem = pl.BlockSpec(memory_space=pltpu.VMEM)
    sem = pltpu.SemaphoreType.DMA
    fine, coarse, wgrad = pl.pallas_call(
        kernel,
        out_shape=(
            jax.ShapeDtypeStruct((NY, NJ, WIDE), BF16),
            jax.ShapeDtypeStruct((COARSE, CIN), BF16),
            jax.ShapeDtypeStruct((NC, NX, QUART, CIN), F32),
        ),
        in_specs=[vmem] * 6,
        out_specs=(vmem, vmem, vmem),
        scratch_shapes=[
            pltpu.VMEM((TAB, CIN), BF16),
            pltpu.VMEM((KVOL * TAB, SLOTS), BF16),
            pltpu.VMEM((CAP * TAB, SLOTS), BF16),
            pltpu.VMEM((ROWS, CIN), BF16),
            pltpu.VMEM((2 * COUT, KVOL * TAB), BF16),
            pltpu.VMEM((ROWS, 2 * TAB), BF16),
            pltpu.VMEM((NY, NJ, WIDE), BF16),
            pltpu.VMEM((NJ, NY, WIDE), BF16),
            pltpu.VMEM((NJ, NY, WIDE), BF16),
            pltpu.VMEM((NJ, NY, WIDE), BF16),
            pltpu.VMEM((NJ, NY, WIDE), BF16),
            pltpu.VMEM((NY, NJ, WIDE), BF16),
            pltpu.VMEM((TAB, CIN), F32),
            pltpu.VMEM((HALO, CIN), F32),
            pltpu.VMEM((HALO, CIN), F32),
            pltpu.VMEM((NC, HALF, CIN), F32),
            pltpu.VMEM((HALF, CIN), F32),
            pltpu.VMEM((NX, QUART, CIN), F32),
            pltpu.VMEM((NX, QUART, CIN), F32),
            pltpu.VMEM((NZ * PART, CIN), F32),
            pltpu.VMEM((NZ, PART, CIN), F32),
            pltpu.VMEM((PART, CIN), F32),
            pltpu.VMEM((NY, PART, CIN), F32),
            pltpu.VMEM((PART, CIN), F32),
            pltpu.VMEM((NZ * PART, CIN), F32),
            pltpu.VMEM((NX, QUART, CIN), F32),
            sem((3, NY)), sem((3, NY)),
            sem((2, NJ)), sem((2, NJ)),
            sem((4,)), sem((4,)),
            sem((2, NZ)), sem((2, NZ)),
            sem((2, NX)), sem((2, NX)),
            sem((2,)), sem((2,)),
        ],
        compiler_params=pltpu.CompilerParams(
            collective_id=0, has_side_effects=True, vmem_limit_bytes=48 * 1024 * 1024
        ),
        cost_estimate=pl.CostEstimate(flops=2_000_000_000, bytes_accessed=4_000_000, transcendentals=0),
    )(
        coarse_features[0],
        child_counts,
        neighbour_rows[0],
        fine_owners.reshape(1, SLOTS),
        weights,
        cotangent.reshape(NY, NJ, WIDE),
    )
    return (
        fine.reshape(1, NS, CAP, COUT),
        coarse[None],
        wgrad.reshape(KVOL, COUT, CIN).transpose(0, 2, 1),
    )


def solution(mesh):
    return jax.shard_map(
        on_device,
        mesh=mesh,
        in_specs=(
            P("scene", "space", None),
            P("scene", "space"),
            P("scene", None, "space"),
            P("scene", "space", None),
            P(),
            P("scene", "space", None, None),
        ),
        out_specs=(P("scene", "space", None, None), P("scene", "space", None), P()),
        check_vma=False,
    )
```

```python
import jax
import jax.numpy as jnp
from jax import lax
from jax.experimental import pallas as pl
from jax.experimental.pallas import tpu as pltpu
from jax.sharding import PartitionSpec as P

KVOL, CIN, COUT = 27, 128, 64
SLOTS, COARSE, HALO, CAP = 512, 64, 16, 6
NY, NZ, NC, NX = 8, 8, 2, 4
NJ = NZ * NC
NS = NY * NJ
TAB = 128
WIDE = CAP * COUT
ROWS = KVOL * COUT
HALF = ROWS // NC
PART = 16
PARTS_B = 3
ROWS_A = NX * NZ * PART
ROWS_B = NZ * PARTS_B * PART
MESH = pl.DeviceIdType.MESH
F32, BF16 = jnp.float32, jnp.bfloat16


def dot(a, b, dims):
    return lax.dot_general(a, b, (dims, ((), ())), preferred_element_type=F32)


def nn(a, b):
    return dot(a, b, ((1,), (0,)))


def nt(a, b):
    return dot(a, b, ((1,), (1,)))


def split(value):
    high = value.astype(BF16)
    return high, (value - high.astype(F32)).astype(BF16)


def iota(shape, dim):
    return lax.broadcasted_iota(jnp.int32, shape, dim)


def kernel(
    feats, counts_in, rows_in, owners_in, wt_in, cot_in,
    fine_out, coarse_out, wgrad_out,
    fine, coarse, out_a, out_b,
    counts, rows, owners, wt, cot,
    table, onehot, place, zz, st,
    c1s, c1, c2s, c2, f1s, f1, f2s, f2,
    grad, rim_low, rim_high,
    core_a, from_core_a, core_b, from_core_b,
    x_a, from_x_a, z_a, from_z_a, y_a, from_y_a, done_a, all_z_a,
    z_b, from_z_b, x_b, from_x_b, y_b, from_y_b, done_b, all_x_b,
    y_send, y_recv, j_send, j_recv, e_send, e_recv,
    z_send, z_recv, x_send, x_recv, p_send, p_recv, in_sems, out_sems,
):
    s, x = lax.axis_index("space"), lax.axis_index("scene")
    y, j = s // NJ, s % NJ
    z, c = j // NC, j % NC
    up, down = (s + 1) % NS, (s + NS - 1) % NS
    partner = y * NJ + z * NC + 1 - c

    def at(space, scene=None):
        return {"space": space, "scene": x if scene is None else scene}

    def y_peer(p):
        return (y + p) % NY

    def j_peer(p):
        return (j + p) % NJ

    def z_peer(p):
        return (z + p) % NZ

    def x_peer(p):
        return (x + p) % NX

    started = []

    def send(src, dst, send_sem, recv_sem, device):
        copy = pltpu.make_async_remote_copy(
            src_ref=src, dst_ref=dst, send_sem=send_sem, recv_sem=recv_sem,
            device_id=device, device_id_type=MESH,
        )
        copy.start()
        started.append(copy)
        return copy

    def over_y(n, src, dst):
        return [
            send(src(y_peer(p)), dst, y_send.at[n, p], y_recv.at[n, p], at(y_peer(p) * NJ + j))
            for p in range(1, NY)
        ]

    def over_j(n, src, dst):
        return [
            send(src(j_peer(p)), dst, j_send.at[n, p], j_recv.at[n, p], at(y * NJ + j_peer(p)))
            for p in range(1, NJ)
        ]

    def over_z(n, src, dst):
        return [
            send(src(z_peer(p)), dst, z_send.at[n, p], z_recv.at[n, p], at(y * NJ + z_peer(p) * NC + c))
            for p in range(1, NZ)
        ]

    def over_x(n, src, dst):
        return [
            send(src(x_peer(p)), dst, x_send.at[n, p], x_recv.at[n, p], at(s, x_peer(p)))
            for p in range(1, NX)
        ]

    def span(ref, i, size):
        return ref.at[pl.ds(pl.multiple_of(i * size, size), size)]

    def arrived(copies):
        for copy in copies:
            copy.wait_recv()

    barrier = pltpu.get_barrier_semaphore()
    peers = [at(y_peer(p) * NJ + j) for p in range(1, NY)]
    peers += [at(y * NJ + j_peer(p)) for p in range(1, NJ)]
    peers += [at(s, x_peer(p)) for p in range(1, NX)]
    peers += [at(up), at(down)]
    for peer in peers:
        pl.semaphore_signal(barrier, inc=1, device_id=peer, device_id_type=MESH)
    loads = [
        pltpu.make_async_copy(src, dst, in_sems.at[i])
        for i, (src, dst) in enumerate((
            (cot_in, cot), (owners_in, owners), (feats, table.at[pl.ds(HALO, COARSE)]),
            (counts_in, counts), (rows_in, rows), (wt_in, wt),
        ))
    ]
    for load in loads:
        load.start()
    table[pl.ds(HALO + COARSE + HALO, TAB - COARSE - 2 * HALO), :] = jnp.zeros(
        (TAB - COARSE - 2 * HALO, CIN), BF16
    )

    def ones(mask):
        return jnp.where(mask, 1.0, 0.0).astype(BF16)

    square = (TAB, TAB)
    loads[0].wait()
    c1s[...] = nt(ones(iota(square, 0) == iota(square, 1)), cot[...]).reshape(NY, NJ, WIDE).astype(BF16)
    line = iota((TAB, SLOTS), 0)
    loads[1].wait()
    named = (line & (NY - 1)) * NJ + (line >> 3) == owners[...]
    earlier = ones(iota((SLOTS, SLOTS), 0) < iota((SLOTS, SLOTS), 1))
    before = nn(ones(named), earlier)
    for r in range(CAP):
        place[pl.ds(r * TAB, TAB), :] = ones(named & (before == r))
    pl.semaphore_wait(barrier, len(peers))

    cot_first = over_y(0, lambda d: c1s.at[d], c1.at[y])
    halo_up = send(
        feats.at[pl.ds(COARSE - HALO, HALO)], table.at[pl.ds(0, HALO)],
        e_send.at[0], e_recv.at[0], at(up),
    )
    halo_down = send(
        feats.at[pl.ds(0, HALO)], table.at[pl.ds(HALO + COARSE, HALO)],
        e_send.at[1], e_recv.at[1], at(down),
    )
    c1[y] = c1s[y]
    for load in loads[2:]:
        load.wait()

    spread = ones(iota((COARSE, SLOTS), 0) == (iota((COARSE, SLOTS), 1) >> 3))
    many = jnp.broadcast_to(counts[...], (8, COARSE)).astype(F32).astype(BF16)
    valid = (iota((1, SLOTS), 1) & 7).astype(F32) < nn(many, spread)[0:1]
    for k in range(KVOL):
        onehot[pl.ds(k * TAB, TAB), :] = ones(line == rows[k])
    to_j = ones(iota(square, 1) == (iota(square, 0) & (NY - 1)) * NJ + (iota(square, 0) >> 3))
    to_y = ones(iota(square, 1) == (iota(square, 0) & (NJ - 1)) * NY + (iota(square, 0) >> 4))

    arrived(cot_first)
    c2s[...] = nn(to_j, c1[...].reshape(NS, WIDE)).reshape(NJ, NY, WIDE).astype(BF16)
    cot_second = over_j(0, lambda d: c2s.at[d], c2.at[j])
    c2[j] = c2s[j]

    arrived([halo_up, halo_down])

    @pl.when(s == 0)
    def _():
        table[pl.ds(0, HALO), :] = jnp.zeros((HALO, CIN), BF16)

    @pl.when(s == NS - 1)
    def _():
        table[pl.ds(HALO + COARSE, HALO), :] = jnp.zeros((HALO, CIN), BF16)

    features = table[...]
    high, low = split(nt(wt[...], features))
    for k in range(KVOL):
        zz[pl.ds(0, COUT), pl.ds(k * TAB, TAB)] = high[k * COUT:(k + 1) * COUT]
        zz[pl.ds(COUT, COUT), pl.ds(k * TAB, TAB)] = low[k * COUT:(k + 1) * COUT]
    both = nn(zz[...], onehot[...])
    slot_out = jnp.where(valid, both[:COUT] + both[COUT:], 0.0).astype(BF16)
    for r in range(CAP):
        f1s[:, :, pl.ds(r * COUT, COUT)] = (
            nt(place[pl.ds(r * TAB, TAB), :], slot_out).reshape(NJ, NY, COUT).astype(BF16)
        )
    fine_first = over_j(1, lambda d: f1s.at[d], f1.at[j])
    f1[j] = f1s[j]

    arrived(cot_second)
    turned = c2[...].astype(F32).reshape(NS, WIDE).T.astype(BF16)
    turned = jnp.concatenate([turned[r * COUT:(r + 1) * COUT] for r in range(CAP)], axis=1)
    slot_grad = jnp.where(valid, nn(turned, place[...]), 0.0).astype(BF16)
    high, low = split(nt(slot_grad, onehot[...]))
    for k in range(KVOL):
        st[pl.ds(k * COUT, COUT), pl.ds(0, TAB)] = high[:, k * TAB:(k + 1) * TAB]
        st[pl.ds(k * COUT, COUT), pl.ds(TAB, TAB)] = low[:, k * TAB:(k + 1) * TAB]
    twice = jnp.concatenate([features, features], axis=0)

    def half(d):
        value = nn(st[pl.ds(pl.multiple_of(d * HALF, 16), HALF), :], twice)
        core_a[d] = value[:ROWS_A].reshape(NX, NZ * PART, CIN)
        rest = jnp.concatenate([value[ROWS_A:], jnp.zeros((ROWS_A + ROWS_B - HALF, CIN), F32)], axis=0)
        core_b[d] = rest.reshape(NZ, PARTS_B * PART, CIN)

    order = (2, 1, 3, 0)
    half(1 - c)
    reduce_core_a = [
        send(core_a.at[1 - c, x_peer(p)], from_core_a.at[x_peer(p)], p_send.at[0, p], p_recv.at[0, p], at(partner))
        for p in order
    ]
    reduce_core_b = send(core_b.at[1 - c], from_core_b, p_send.at[0, NX], p_recv.at[0, NX], at(partner))
    half(c)
    reduce_x_a = []
    for p, copy in zip(order, reduce_core_a):
        arrived([copy])
        d = x_peer(p)
        x_a[d] = core_a[c, d] + from_core_a[d]
        if p:
            reduce_x_a.append(send(x_a.at[d], from_x_a.at[x], x_send.at[0, p], x_recv.at[0, p], at(s, d)))
    arrived([reduce_core_b])
    z_b[...] = core_b[c] + from_core_b[...]
    reduce_z_b = over_z(0, lambda d: z_b.at[d], from_z_b.at[z])

    total = dot(st[...], wt[...], ((0,), (0,)))
    grad[...] = total[:TAB] + total[TAB:]
    rim_down = send(grad.at[pl.ds(0, HALO)], rim_high, e_send.at[2], e_recv.at[2], at(down))
    rim_up = send(
        grad.at[pl.ds(HALO + COARSE, HALO)], rim_low, e_send.at[3], e_recv.at[3], at(up)
    )
    x_b[NX - 1] = jnp.zeros((PART, CIN), F32)

    arrived(reduce_x_a)
    mine = x_a[x]
    for p in range(1, NX):
        mine = mine + from_x_a[x_peer(p)]
    z_a[...] = mine.reshape(NZ, PART, CIN)
    reduce_z_a = over_z(1, lambda d: z_a.at[d], from_z_a.at[z])

    arrived(reduce_z_b)
    mine = z_b[z]
    for p in range(1, NZ):
        mine = mine + from_z_b[z_peer(p)]
    x_b[pl.ds(0, PARTS_B)] = mine.reshape(PARTS_B, PART, CIN)
    reduce_x_b = over_x(1, lambda d: x_b.at[d], from_x_b.at[x])

    arrived(fine_first)
    f2s[...] = (
        nn(to_y, f1[...].astype(F32).reshape(NS, WIDE).astype(BF16)).astype(BF16).reshape(NY, NJ, WIDE)
    )
    fine_second = over_y(1, lambda d: f2s.at[d], f2.at[y])
    f2[y] = f2s[y]

    arrived(reduce_z_a)
    mine = z_a[z]
    for p in range(1, NZ):
        mine = mine + from_z_a[z_peer(p)]
    y_a[...] = mine
    exchange_y_a = over_y(2, lambda d: y_a, from_y_a.at[y])
    from_y_a[y] = mine

    arrived(reduce_x_b)
    mine = x_b[x]
    for p in range(1, NX):
        mine = mine + from_x_b[x_peer(p)]
    y_b[...] = mine
    exchange_y_b = over_y(3, lambda d: y_b, from_y_b.at[y])
    from_y_b[y] = mine

    arrived([rim_down, rim_up])
    own = grad[pl.ds(HALO, COARSE), :]
    low = rim_low[...] * jnp.where(s == 0, 0.0, 1.0)
    high = rim_high[...] * jnp.where(s == NS - 1, 0.0, 1.0)
    coarse[pl.ds(0, HALO), :] = (own[:HALO] + low).astype(BF16)
    coarse[pl.ds(HALO, COARSE - 2 * HALO), :] = own[HALO:COARSE - HALO].astype(BF16)
    coarse[pl.ds(COARSE - HALO, HALO), :] = (own[COARSE - HALO:] + high).astype(BF16)
    stores = []

    def store(src, dst):
        copy = pltpu.make_async_copy(src, dst, out_sems.at[len(stores)])
        copy.start()
        stores.append(copy)

    store(coarse, coarse_out)

    arrived(exchange_y_a)
    done = from_y_a[0]
    for q in range(1, NY):
        done = done + from_y_a[q]
    done_a[...] = done
    gather_z_a = over_z(2, lambda d: done_a, span(all_z_a, z, PART))
    span(all_z_a, z, PART)[...] = done

    arrived(exchange_y_b)
    done = from_y_b[0]
    for q in range(1, NY):
        done = done + from_y_b[q]
    done_b[...] = done
    gather_x_b = over_x(2, lambda d: done_b, span(all_x_b, x, PART))
    span(all_x_b, x, PART)[...] = done

    arrived(fine_second)
    fine[...] = f2[...].astype(F32).reshape(NS, WIDE).T.astype(BF16)
    store(fine, fine_out)

    arrived(gather_x_b)
    wide_a, wide_b = NZ * PART, PARTS_B * PART
    whole_b = all_x_b.at[pl.ds(0, wide_b)]
    gather_z_b = over_z(3, lambda d: whole_b, span(out_b.at[c], z, wide_b))
    gather_core = [send(whole_b, span(out_b.at[c], z, wide_b), p_send.at[1, NX], p_recv.at[1, NX], at(partner))]
    span(out_b.at[c], z, wide_b)[...] = whole_b[...]

    arrived(gather_z_a)
    gather_x_a = over_x(3, lambda d: all_z_a, span(out_a.at[c], x, wide_a))
    gather_core.append(send(all_z_a, span(out_a.at[c], x, wide_a), p_send.at[1, 0], p_recv.at[1, 0], at(partner)))
    span(out_a.at[c], x, wide_a)[...] = all_z_a[...]
    for p in (1, 7, 2, 6, 3, 5, 4):
        arrived([gather_z_b[p - 1]])
        piece = span(out_b.at[c], (z + NZ - p) % NZ, wide_b)
        gather_core.append(send(piece, piece, p_send.at[1, NX + p], p_recv.at[1, NX + p], at(partner)))
    for p in (1, 3, 2):
        arrived([gather_x_a[p - 1]])
        piece = span(out_a.at[c], (x + NX - p) % NX, wide_a)
        gather_core.append(send(piece, piece, p_send.at[1, p], p_recv.at[1, p], at(partner)))

    def store_half(d):
        store(out_a.at[d], wgrad_out.at[d, pl.ds(0, ROWS_A)])
        store(out_b.at[d, pl.ds(0, HALF - ROWS_A)], wgrad_out.at[d, pl.ds(ROWS_A, HALF - ROWS_A)])

    store_half(c)
    arrived(gather_core)
    store_half(1 - c)
    for copy in started:
        copy.wait_send()
    for copy in stores:
        copy.wait()


def finish_kernel(fine, coarse, wgrad, fine_out, coarse_out, wgrad_out, fine_v, coarse_v, wgrad_v, sems):
    quarter = HALF // 2
    trips = [(coarse, coarse_v, coarse_out), (fine, fine_v, fine_out)]
    for c in range(NC):
        for q in range(2):
            rows = pl.ds(q * quarter, quarter)
            trips.append(tuple(ref.at[c, rows] for ref in (wgrad, wgrad_v, wgrad_out)))
    loads = [pltpu.make_async_copy(a, b, sems.at[0, i]) for i, (a, b, _) in enumerate(trips)]
    stores = [pltpu.make_async_copy(b, c, sems.at[1, i]) for i, (_, b, c) in enumerate(trips)]
    for load in loads:
        load.start()
    for load, copy in zip(loads, stores):
        load.wait()
        copy.start()
    for copy in stores:
        copy.wait()


def on_device(coarse_features, child_counts, neighbour_rows, fine_owners, weights, cotangent):
    sem = pltpu.SemaphoreType.DMA
    hbm = pl.BlockSpec(memory_space=pltpu.HBM)
    fine, coarse, wgrad = pl.pallas_call(
        kernel,
        out_shape=(
            jax.ShapeDtypeStruct((WIDE, NS), BF16),
            jax.ShapeDtypeStruct((COARSE, CIN), BF16),
            jax.ShapeDtypeStruct((NC, HALF, CIN), F32),
        ),
        in_specs=[hbm] * 6,
        out_specs=(hbm,) * 3,
        scratch_shapes=[
            pltpu.VMEM((WIDE, NS), BF16),
            pltpu.VMEM((COARSE, CIN), BF16),
            pltpu.VMEM((NC, ROWS_A, CIN), F32),
            pltpu.VMEM((NC, ROWS_B, CIN), F32),
            pltpu.VMEM((1, COARSE), jnp.int32),
            pltpu.VMEM((KVOL, 1, SLOTS), jnp.int32),
            pltpu.VMEM((1, SLOTS), jnp.int32),
            pltpu.VMEM((ROWS, CIN), BF16),
            pltpu.VMEM((WIDE, NS), BF16),
            pltpu.VMEM((TAB, CIN), BF16),
            pltpu.VMEM((KVOL * TAB, SLOTS), BF16),
            pltpu.VMEM((CAP * TAB, SLOTS), BF16),
            pltpu.VMEM((2 * COUT, KVOL * TAB), BF16),
            pltpu.VMEM((ROWS, 2 * TAB), BF16),
            pltpu.VMEM((NY, NJ, WIDE), BF16),
            pltpu.VMEM((NY, NJ, WIDE), BF16),
            pltpu.VMEM((NJ, NY, WIDE), BF16),
            pltpu.VMEM((NJ, NY, WIDE), BF16),
            pltpu.VMEM((NJ, NY, WIDE), BF16),
            pltpu.VMEM((NJ, NY, WIDE), BF16),
            pltpu.VMEM((NY, NJ, WIDE), BF16),
            pltpu.VMEM((NY, NJ, WIDE), BF16),
            pltpu.VMEM((TAB, CIN), F32),
            pltpu.VMEM((HALO, CIN), F32),
            pltpu.VMEM((HALO, CIN), F32),
            pltpu.VMEM((NC, NX, NZ * PART, CIN), F32),
            pltpu.VMEM((NX, NZ * PART, CIN), F32),
            pltpu.VMEM((NC, NZ, PARTS_B * PART, CIN), F32),
            pltpu.VMEM((NZ, PARTS_B * PART, CIN), F32),
            pltpu.VMEM((NX, NZ * PART, CIN), F32),
            pltpu.VMEM((NX, NZ * PART, CIN), F32),
            pltpu.VMEM((NZ, PART, CIN), F32),
            pltpu.VMEM((NZ, PART, CIN), F32),
            pltpu.VMEM((PART, CIN), F32),
            pltpu.VMEM((NY, PART, CIN), F32),
            pltpu.VMEM((PART, CIN), F32),
            pltpu.VMEM((NZ * PART, CIN), F32),
            pltpu.VMEM((NZ, PARTS_B * PART, CIN), F32),
            pltpu.VMEM((NZ, PARTS_B * PART, CIN), F32),
            pltpu.VMEM((NX, PART, CIN), F32),
            pltpu.VMEM((NX, PART, CIN), F32),
            pltpu.VMEM((PART, CIN), F32),
            pltpu.VMEM((NY, PART, CIN), F32),
            pltpu.VMEM((PART, CIN), F32),
            pltpu.VMEM((NX * PART, CIN), F32),
            sem((4, NY)), sem((4, NY)),
            sem((2, NJ)), sem((2, NJ)),
            sem((4,)), sem((4,)),
            sem((4, NZ)), sem((4, NZ)),
            sem((4, NX)), sem((4, NX)),
            sem((2, NX + NZ)), sem((2, NX + NZ)),
            sem((6,)), sem((6,)),
        ],
        compiler_params=pltpu.CompilerParams(
            collective_id=0, has_side_effects=True, vmem_limit_bytes=58000 * 1024
        ),
        cost_estimate=pl.CostEstimate(flops=2_000_000_000, bytes_accessed=4_000_000, transcendentals=0),
    )(
        coarse_features[0],
        child_counts,
        neighbour_rows.reshape(KVOL, 1, SLOTS),
        fine_owners.reshape(1, SLOTS),
        weights.transpose(0, 2, 1).reshape(ROWS, CIN),
        cotangent[0].transpose(1, 2, 0).reshape(WIDE, NS),
    )
    fine, coarse, wgrad = pl.pallas_call(
        finish_kernel,
        out_shape=(
            jax.ShapeDtypeStruct((WIDE, NS), BF16),
            jax.ShapeDtypeStruct((COARSE, CIN), BF16),
            jax.ShapeDtypeStruct((NC, HALF, CIN), F32),
        ),
        in_specs=[hbm] * 3,
        out_specs=(hbm,) * 3,
        scratch_shapes=[
            pltpu.VMEM((WIDE, NS), BF16),
            pltpu.VMEM((COARSE, CIN), BF16),
            pltpu.VMEM((NC, HALF, CIN), F32),
            sem((2, 6)),
        ],
        compiler_params=pltpu.CompilerParams(vmem_limit_bytes=58000 * 1024),
    )(fine, coarse, wgrad)
    return (
        fine.reshape(CAP, COUT, NS).transpose(2, 0, 1)[None],
        coarse[None],
        wgrad.reshape(KVOL, COUT, CIN).transpose(0, 2, 1),
    )


def solution(mesh):
    return jax.shard_map(
        on_device,
        mesh=mesh,
        in_specs=(
            P("scene", "space", None),
            P("scene", "space"),
            P("scene", None, "space"),
            P("scene", "space", None),
            P(),
            P("scene", "space", None, None),
        ),
        out_specs=(P("scene", "space", None, None), P("scene", "space", None), P()),
        check_vma=False,
    )
```

```python
import jax
import jax.numpy as jnp
from jax import lax
from jax.experimental import pallas as pl
from jax.experimental.pallas import tpu as pltpu
from jax.sharding import PartitionSpec as P

KVOL, CIN, COUT = 27, 128, 64
SLOTS, COARSE, HALO, CAP = 512, 64, 16, 6
NY, NZ, NC, NX = 8, 8, 2, 4
NJ = NZ * NC
NS = NY * NJ
TAB = 128
WIDE = CAP * COUT
ROWS = KVOL * COUT
HALF = ROWS // NC
PART = 16
PARTS_B = 3
ROWS_A = NX * NZ * PART
ROWS_B = NZ * PARTS_B * PART
MESH = pl.DeviceIdType.MESH
F32, BF16 = jnp.float32, jnp.bfloat16


def dot(a, b, dims):
    return lax.dot_general(a, b, (dims, ((), ())), preferred_element_type=F32)


def nn(a, b):
    return dot(a, b, ((1,), (0,)))


def nt(a, b):
    return dot(a, b, ((1,), (1,)))


def split(value):
    high = value.astype(BF16)
    return high, (value - high.astype(F32)).astype(BF16)


def iota(shape, dim):
    return lax.broadcasted_iota(jnp.int32, shape, dim)


def far_first(n):
    return sorted(range(1, n), key=lambda p: -min(p, n - p))


def kernel(
    feats, counts_in, rows_in, owners_in, wt_in, cot_in,
    fine, coarse, out_a, out_b,
    counts, rows, owners, wt, cot,
    table, onehot, place, zz, st,
    c1s, c1, c2s, c2, f1s, f1, f2s, f2,
    grad, rim_low, rim_high,
    core_a, from_core_a, core_b, from_core_b,
    x_a, from_x_a, z_a, from_z_a, y_a, from_y_a, done_a, all_z_a,
    z_b, from_z_b, x_b, from_x_b, y_b, from_y_b, done_b, all_x_b,
    y_send, y_recv, j_send, j_recv, e_send, e_recv,
    z_send, z_recv, x_send, x_recv, p_send, p_recv, in_sems,
):
    s, x = lax.axis_index("space"), lax.axis_index("scene")
    y, j = s // NJ, s % NJ
    z, c = j // NC, j % NC
    up, down = (s + 1) % NS, (s + NS - 1) % NS
    partner = y * NJ + z * NC + 1 - c

    def at(space, scene=None):
        return {"space": space, "scene": x if scene is None else scene}

    def y_peer(p):
        return (y + p) % NY

    def j_peer(p):
        return (j + p) % NJ

    def z_peer(p):
        return (z + p) % NZ

    def x_peer(p):
        return (x + p) % NX

    started = []

    def send(src, dst, send_sem, recv_sem, device):
        copy = pltpu.make_async_remote_copy(
            src_ref=src, dst_ref=dst, send_sem=send_sem, recv_sem=recv_sem,
            device_id=device, device_id_type=MESH,
        )
        copy.start()
        started.append(copy)
        return copy

    def over_y(n, src, dst):
        return {
            p: send(src(y_peer(p)), dst, y_send.at[n, p], y_recv.at[n, p], at(y_peer(p) * NJ + j))
            for p in far_first(NY)
        }

    def over_j(n, src, dst):
        return {
            p: send(src(j_peer(p)), dst, j_send.at[n, p], j_recv.at[n, p], at(y * NJ + j_peer(p)))
            for p in far_first(NJ)
        }

    def over_z(n, src, dst):
        return {
            p: send(src(z_peer(p)), dst, z_send.at[n, p], z_recv.at[n, p], at(y * NJ + z_peer(p) * NC + c))
            for p in far_first(NZ)
        }

    def over_x(n, src, dst):
        return {
            p: send(src(x_peer(p)), dst, x_send.at[n, p], x_recv.at[n, p], at(s, x_peer(p)))
            for p in far_first(NX)
        }

    def span(ref, i, size):
        return ref.at[pl.ds(pl.multiple_of(i * size, size), size)]

    def arrived(copies):
        for copy in copies.values() if isinstance(copies, dict) else copies:
            copy.wait_recv()

    barrier = pltpu.get_barrier_semaphore()
    peers = [at(y_peer(p) * NJ + j) for p in range(1, NY)]
    peers += [at(y * NJ + j_peer(p)) for p in range(1, NJ)]
    peers += [at(s, x_peer(p)) for p in range(1, NX)]
    peers += [at(up), at(down)]
    for peer in peers:
        pl.semaphore_signal(barrier, inc=1, device_id=peer, device_id_type=MESH)
    loads = [
        pltpu.make_async_copy(src, dst, in_sems.at[i])
        for i, (src, dst) in enumerate((
            (cot_in, cot), (owners_in, owners), (feats, table.at[pl.ds(HALO, COARSE)]),
            (counts_in, counts), (rows_in, rows), (wt_in, wt),
        ))
    ]
    for load in loads:
        load.start()
    table[pl.ds(HALO + COARSE + HALO, TAB - COARSE - 2 * HALO), :] = jnp.zeros(
        (TAB - COARSE - 2 * HALO, CIN), BF16
    )

    def ones(mask):
        return jnp.where(mask, 1.0, 0.0).astype(BF16)

    square = (TAB, TAB)
    loads[0].wait()
    c1s[...] = nt(ones(iota(square, 0) == iota(square, 1)), cot[...]).reshape(NY, NJ, WIDE).astype(BF16)
    pl.semaphore_wait(barrier, len(peers))

    cot_first = over_y(0, lambda d: c1s.at[d], c1.at[y])
    halo_up = send(
        feats.at[pl.ds(COARSE - HALO, HALO)], table.at[pl.ds(0, HALO)],
        e_send.at[0], e_recv.at[0], at(up),
    )
    halo_down = send(
        feats.at[pl.ds(0, HALO)], table.at[pl.ds(HALO + COARSE, HALO)],
        e_send.at[1], e_recv.at[1], at(down),
    )
    c1[y] = c1s[y]
    for load in loads[1:]:
        load.wait()
    line = iota((TAB, SLOTS), 0)
    named = (line & (NY - 1)) * NJ + (line >> 3) == owners[...]
    earlier = ones(iota((SLOTS, SLOTS), 0) < iota((SLOTS, SLOTS), 1))
    before = nn(ones(named), earlier)
    for r in range(CAP):
        place[pl.ds(r * TAB, TAB), :] = ones(named & (before == r))

    spread = ones(iota((COARSE, SLOTS), 0) == (iota((COARSE, SLOTS), 1) >> 3))
    many = jnp.broadcast_to(counts[...], (8, COARSE)).astype(F32).astype(BF16)
    valid = (iota((1, SLOTS), 1) & 7).astype(F32) < nn(many, spread)[0:1]
    for k in range(KVOL):
        onehot[pl.ds(k * TAB, TAB), :] = ones(line == rows[k])
    to_j = ones(iota(square, 1) == (iota(square, 0) & (NY - 1)) * NJ + (iota(square, 0) >> 3))
    to_y = ones(iota(square, 1) == (iota(square, 0) & (NJ - 1)) * NY + (iota(square, 0) >> 4))

    arrived(cot_first)
    c2s[...] = nn(to_j, c1[...].reshape(NS, WIDE)).reshape(NJ, NY, WIDE).astype(BF16)
    cot_second = over_j(0, lambda d: c2s.at[d], c2.at[j])
    c2[j] = c2s[j]

    arrived([halo_up, halo_down])

    @pl.when(s == 0)
    def _():
        table[pl.ds(0, HALO), :] = jnp.zeros((HALO, CIN), BF16)

    @pl.when(s == NS - 1)
    def _():
        table[pl.ds(HALO + COARSE, HALO), :] = jnp.zeros((HALO, CIN), BF16)

    features = table[...]
    high, low = split(nt(wt[...], features))
    for k in range(KVOL):
        zz[pl.ds(0, COUT), pl.ds(k * TAB, TAB)] = high[k * COUT:(k + 1) * COUT]
        zz[pl.ds(COUT, COUT), pl.ds(k * TAB, TAB)] = low[k * COUT:(k + 1) * COUT]
    both = nn(zz[...], onehot[...])
    slot_out = jnp.where(valid, both[:COUT] + both[COUT:], 0.0).astype(BF16)
    for r in range(CAP):
        f1s[:, :, pl.ds(r * COUT, COUT)] = (
            nt(place[pl.ds(r * TAB, TAB), :], slot_out).reshape(NJ, NY, COUT).astype(BF16)
        )
    fine_first = over_j(1, lambda d: f1s.at[d], f1.at[j])
    f1[j] = f1s[j]

    arrived(cot_second)
    turned = c2[...].astype(F32).reshape(NS, WIDE).T.astype(BF16)
    turned = jnp.concatenate([turned[r * COUT:(r + 1) * COUT] for r in range(CAP)], axis=1)
    slot_grad = jnp.where(valid, nn(turned, place[...]), 0.0).astype(BF16)
    high, low = split(nt(slot_grad, onehot[...]))
    for k in range(KVOL):
        st[pl.ds(k * COUT, COUT), pl.ds(0, TAB)] = high[:, k * TAB:(k + 1) * TAB]
        st[pl.ds(k * COUT, COUT), pl.ds(TAB, TAB)] = low[:, k * TAB:(k + 1) * TAB]
    twice = jnp.concatenate([features, features], axis=0)

    def half(d):
        value = nn(st[pl.ds(pl.multiple_of(d * HALF, 16), HALF), :], twice)
        core_a[d] = value[:ROWS_A].reshape(NX, NZ * PART, CIN)
        rest = jnp.concatenate([value[ROWS_A:], jnp.zeros((ROWS_A + ROWS_B - HALF, CIN), F32)], axis=0)
        core_b[d] = rest.reshape(NZ, PARTS_B * PART, CIN)

    order = (2, 1, 3, 0)
    half(1 - c)
    reduce_core_a = [
        send(core_a.at[1 - c, x_peer(p)], from_core_a.at[x_peer(p)], p_send.at[0, p], p_recv.at[0, p], at(partner))
        for p in order
    ]
    reduce_core_b = send(core_b.at[1 - c], from_core_b, p_send.at[0, NX], p_recv.at[0, NX], at(partner))
    half(c)
    reduce_x_a = []
    for p, copy in zip(order, reduce_core_a):
        arrived([copy])
        d = x_peer(p)
        x_a[d] = core_a[c, d] + from_core_a[d]
        if p:
            reduce_x_a.append(send(x_a.at[d], from_x_a.at[x], x_send.at[0, p], x_recv.at[0, p], at(s, d)))
    arrived([reduce_core_b])
    z_b[...] = core_b[c] + from_core_b[...]
    reduce_z_b = over_z(0, lambda d: z_b.at[d], from_z_b.at[z])

    total = dot(st[...], wt[...], ((0,), (0,)))
    grad[...] = total[:TAB] + total[TAB:]
    rim_down = send(grad.at[pl.ds(0, HALO)], rim_high, e_send.at[2], e_recv.at[2], at(down))
    rim_up = send(
        grad.at[pl.ds(HALO + COARSE, HALO)], rim_low, e_send.at[3], e_recv.at[3], at(up)
    )
    x_b[NX - 1] = jnp.zeros((PART, CIN), F32)

    arrived(reduce_x_a)
    mine = x_a[x]
    for p in range(1, NX):
        mine = mine + from_x_a[x_peer(p)]
    z_a[...] = mine.reshape(NZ, PART, CIN)
    reduce_z_a = over_z(1, lambda d: z_a.at[d], from_z_a.at[z])

    arrived(reduce_z_b)
    mine = z_b[z]
    for p in range(1, NZ):
        mine = mine + from_z_b[z_peer(p)]
    x_b[pl.ds(0, PARTS_B)] = mine.reshape(PARTS_B, PART, CIN)
    reduce_x_b = over_x(1, lambda d: x_b.at[d], from_x_b.at[x])

    arrived(fine_first)
    f2s[...] = (
        nn(to_y, f1[...].astype(F32).reshape(NS, WIDE).astype(BF16)).astype(BF16).reshape(NY, NJ, WIDE)
    )
    fine_second = over_y(1, lambda d: f2s.at[d], f2.at[y])
    f2[y] = f2s[y]

    arrived(reduce_z_a)
    mine = z_a[z]
    for p in range(1, NZ):
        mine = mine + from_z_a[z_peer(p)]
    y_a[...] = mine
    exchange_y_a = over_y(2, lambda d: y_a, from_y_a.at[y])
    from_y_a[y] = mine

    arrived(reduce_x_b)
    mine = x_b[x]
    for p in range(1, NX):
        mine = mine + from_x_b[x_peer(p)]
    y_b[...] = mine
    exchange_y_b = over_y(3, lambda d: y_b, from_y_b.at[y])
    from_y_b[y] = mine

    arrived([rim_down, rim_up])
    own = grad[pl.ds(HALO, COARSE), :]
    low = rim_low[...] * jnp.where(s == 0, 0.0, 1.0)
    high = rim_high[...] * jnp.where(s == NS - 1, 0.0, 1.0)
    coarse[pl.ds(0, HALO), :] = (own[:HALO] + low).astype(BF16)
    coarse[pl.ds(HALO, COARSE - 2 * HALO), :] = own[HALO:COARSE - HALO].astype(BF16)
    coarse[pl.ds(COARSE - HALO, HALO), :] = (own[COARSE - HALO:] + high).astype(BF16)

    arrived(exchange_y_a)
    done = from_y_a[0]
    for q in range(1, NY):
        done = done + from_y_a[q]
    done_a[...] = done
    gather_z_a = over_z(2, lambda d: done_a, span(all_z_a, z, PART))
    span(all_z_a, z, PART)[...] = done

    arrived(exchange_y_b)
    done = from_y_b[0]
    for q in range(1, NY):
        done = done + from_y_b[q]
    done_b[...] = done
    gather_x_b = over_x(2, lambda d: done_b, span(all_x_b, x, PART))
    span(all_x_b, x, PART)[...] = done

    arrived(fine_second)
    fine[...] = f2[...].astype(F32).reshape(NS, WIDE).T.astype(BF16)

    arrived(gather_x_b)
    wide_a, wide_b = NZ * PART, PARTS_B * PART
    whole_b = all_x_b.at[pl.ds(0, wide_b)]
    gather_z_b = over_z(3, lambda d: whole_b, span(out_b.at[c], z, wide_b))
    gather_core = [send(whole_b, span(out_b.at[c], z, wide_b), p_send.at[1, NX], p_recv.at[1, NX], at(partner))]
    span(out_b.at[c], z, wide_b)[...] = whole_b[...]

    arrived(gather_z_a)
    gather_x_a = over_x(3, lambda d: all_z_a, span(out_a.at[c], x, wide_a))
    gather_core.append(send(all_z_a, span(out_a.at[c], x, wide_a), p_send.at[1, 0], p_recv.at[1, 0], at(partner)))
    span(out_a.at[c], x, wide_a)[...] = all_z_a[...]
    for p in (1, 7, 2, 6, 3, 5, 4):
        arrived([gather_z_b[p]])
        piece = span(out_b.at[c], (z + NZ - p) % NZ, wide_b)
        gather_core.append(send(piece, piece, p_send.at[1, NX + p], p_recv.at[1, NX + p], at(partner)))
    for p in (1, 3, 2):
        arrived([gather_x_a[p]])
        piece = span(out_a.at[c], (x + NX - p) % NX, wide_a)
        gather_core.append(send(piece, piece, p_send.at[1, p], p_recv.at[1, p], at(partner)))
    arrived(gather_core)
    for copy in started:
        copy.wait_send()


def finish_kernel(fine, coarse, part_a, part_b, fine_out, coarse_out, wgrad_out, sems):
    pairs = [(fine, fine_out), (coarse, coarse_out)]
    for c in range(NC):
        pairs.append((part_a.at[c], wgrad_out.at[c, pl.ds(0, ROWS_A)]))
        pairs.append((part_b.at[c, pl.ds(0, HALF - ROWS_A)], wgrad_out.at[c, pl.ds(ROWS_A, HALF - ROWS_A)]))
    copies = [pltpu.make_async_copy(src, dst, sems.at[i]) for i, (src, dst) in enumerate(pairs)]
    for copy in copies:
        copy.start()
    for copy in copies:
        copy.wait()


def on_device(coarse_features, child_counts, neighbour_rows, fine_owners, weights, cotangent):
    sem = pltpu.SemaphoreType.DMA
    vmem = pl.BlockSpec(memory_space=pltpu.VMEM)
    hbm = pl.BlockSpec(memory_space=pltpu.HBM)
    fine, coarse, part_a, part_b = pl.pallas_call(
        kernel,
        out_shape=(
            jax.ShapeDtypeStruct((WIDE, NS), BF16),
            jax.ShapeDtypeStruct((COARSE, CIN), BF16),
            jax.ShapeDtypeStruct((NC, ROWS_A, CIN), F32),
            jax.ShapeDtypeStruct((NC, ROWS_B, CIN), F32),
        ),
        in_specs=[hbm] * 6,
        out_specs=(vmem,) * 4,
        scratch_shapes=[
            pltpu.VMEM((1, COARSE), jnp.int32),
            pltpu.VMEM((KVOL, 1, SLOTS), jnp.int32),
            pltpu.VMEM((1, SLOTS), jnp.int32),
            pltpu.VMEM((ROWS, CIN), BF16),
            pltpu.VMEM((WIDE, NS), BF16),
            pltpu.VMEM((TAB, CIN), BF16),
            pltpu.VMEM((KVOL * TAB, SLOTS), BF16),
            pltpu.VMEM((CAP * TAB, SLOTS), BF16),
            pltpu.VMEM((2 * COUT, KVOL * TAB), BF16),
            pltpu.VMEM((ROWS, 2 * TAB), BF16),
            pltpu.VMEM((NY, NJ, WIDE), BF16),
            pltpu.VMEM((NY, NJ, WIDE), BF16),
            pltpu.VMEM((NJ, NY, WIDE), BF16),
            pltpu.VMEM((NJ, NY, WIDE), BF16),
            pltpu.VMEM((NJ, NY, WIDE), BF16),
            pltpu.VMEM((NJ, NY, WIDE), BF16),
            pltpu.VMEM((NY, NJ, WIDE), BF16),
            pltpu.VMEM((NY, NJ, WIDE), BF16),
            pltpu.VMEM((TAB, CIN), F32),
            pltpu.VMEM((HALO, CIN), F32),
            pltpu.VMEM((HALO, CIN), F32),
            pltpu.VMEM((NC, NX, NZ * PART, CIN), F32),
            pltpu.VMEM((NX, NZ * PART, CIN), F32),
            pltpu.VMEM((NC, NZ, PARTS_B * PART, CIN), F32),
            pltpu.VMEM((NZ, PARTS_B * PART, CIN), F32),
            pltpu.VMEM((NX, NZ * PART, CIN), F32),
            pltpu.VMEM((NX, NZ * PART, CIN), F32),
            pltpu.VMEM((NZ, PART, CIN), F32),
            pltpu.VMEM((NZ, PART, CIN), F32),
            pltpu.VMEM((PART, CIN), F32),
            pltpu.VMEM((NY, PART, CIN), F32),
            pltpu.VMEM((PART, CIN), F32),
            pltpu.VMEM((NZ * PART, CIN), F32),
            pltpu.VMEM((NZ, PARTS_B * PART, CIN), F32),
            pltpu.VMEM((NZ, PARTS_B * PART, CIN), F32),
            pltpu.VMEM((NX, PART, CIN), F32),
            pltpu.VMEM((NX, PART, CIN), F32),
            pltpu.VMEM((PART, CIN), F32),
            pltpu.VMEM((NY, PART, CIN), F32),
            pltpu.VMEM((PART, CIN), F32),
            pltpu.VMEM((NX * PART, CIN), F32),
            sem((4, NY)), sem((4, NY)),
            sem((2, NJ)), sem((2, NJ)),
            sem((4,)), sem((4,)),
            sem((4, NZ)), sem((4, NZ)),
            sem((4, NX)), sem((4, NX)),
            sem((2, NX + NZ)), sem((2, NX + NZ)),
            sem((6,)),
        ],
        compiler_params=pltpu.CompilerParams(
            collective_id=0, has_side_effects=True, vmem_limit_bytes=48 * 1024 * 1024
        ),
        cost_estimate=pl.CostEstimate(flops=2_000_000_000, bytes_accessed=4_000_000, transcendentals=0),
    )(*(
        pltpu.with_memory_space_constraint(operand, pltpu.HBM)
        for operand in (
            coarse_features[0],
            child_counts,
            neighbour_rows.reshape(KVOL, 1, SLOTS),
            fine_owners.reshape(1, SLOTS),
            weights.transpose(0, 2, 1).reshape(ROWS, CIN),
            cotangent[0].transpose(1, 2, 0).reshape(WIDE, NS),
        )
    ))
    fine, coarse, wgrad = pl.pallas_call(
        finish_kernel,
        out_shape=(
            jax.ShapeDtypeStruct((WIDE, NS), BF16),
            jax.ShapeDtypeStruct((COARSE, CIN), BF16),
            jax.ShapeDtypeStruct((NC, HALF, CIN), F32),
        ),
        in_specs=[vmem] * 4,
        out_specs=(hbm,) * 3,
        scratch_shapes=[sem((6,))],
        compiler_params=pltpu.CompilerParams(vmem_limit_bytes=4 * 1024 * 1024),
    )(fine, coarse, part_a, part_b)
    return (
        fine.reshape(CAP, COUT, NS).transpose(2, 0, 1)[None],
        coarse[None],
        wgrad.reshape(KVOL, COUT, CIN).transpose(0, 2, 1),
    )


def solution(mesh):
    return jax.shard_map(
        on_device,
        mesh=mesh,
        in_specs=(
            P("scene", "space", None),
            P("scene", "space"),
            P("scene", None, "space"),
            P("scene", "space", None),
            P(),
            P("scene", "space", None, None),
        ),
        out_specs=(P("scene", "space", None, None), P("scene", "space", None), P()),
        check_vma=False,
    )
```

```python
import jax
import jax.numpy as jnp
from jax import lax
from jax.experimental import pallas as pl
from jax.experimental.pallas import tpu as pltpu
from jax.sharding import PartitionSpec as P

KVOL, CIN, COUT = 27, 128, 64
SLOTS, COARSE, HALO, CAP = 512, 64, 16, 6
NY, NZ, NC, NX = 8, 8, 2, 4
NJ = NZ * NC
NS = NY * NJ
TAB = 128
WIDE = CAP * COUT
ROWS = KVOL * COUT
KHALF = (KVOL + 1) // NC
HALF = KHALF * COUT
PART = 16
PARTS_B = 3
ROWS_A = NX * NZ * PART
ROWS_B = NZ * PARTS_B * PART
MESH = pl.DeviceIdType.MESH
F32, BF16 = jnp.float32, jnp.bfloat16


def dot(a, b, dims):
    return lax.dot_general(a, b, (dims, ((), ())), preferred_element_type=F32)


def nn(a, b):
    return dot(a, b, ((1,), (0,)))


def nt(a, b):
    return dot(a, b, ((1,), (1,)))


def split(value):
    high = value.astype(BF16)
    return high, (value - high.astype(F32)).astype(BF16)


def iota(shape, dim):
    return lax.broadcasted_iota(jnp.int32, shape, dim)


def far_first(n):
    return sorted(range(1, n), key=lambda p: -min(p, n - p))


def kernel(
    feats, counts_in, rows_in, owners_in, wt_in, cot_in,
    fine, coarse, out_a, out_b,
    counts, rows, owners, wt, cot,
    table, onehot, place, found, st,
    c1s, c1, c2s, c2, f1s, f1, f2s, f2,
    grad, rim_low, rim_high,
    core_a, from_core_a, core_b, from_core_b,
    x_a, from_x_a, z_a, from_z_a, y_a, from_y_a, done_a, all_z_a,
    y_b, from_y_b, x_b, from_x_b, z_b, from_z_b, done_b, all_x_b,
    y_send, y_recv, j_send, j_recv, e_send, e_recv,
    z_send, z_recv, x_send, x_recv, p_send, p_recv, in_sems,
):
    s, x = lax.axis_index("space"), lax.axis_index("scene")
    y, j = s // NJ, s % NJ
    z, c = j // NC, j % NC
    up, down = (s + 1) % NS, (s + NS - 1) % NS
    partner = y * NJ + z * NC + 1 - c

    def at(space, scene=None):
        return {"space": space, "scene": x if scene is None else scene}

    def y_peer(p):
        return (y + p) % NY

    def j_peer(p):
        return (j + p) % NJ

    def z_peer(p):
        return (z + p) % NZ

    def x_peer(p):
        return (x + p) % NX

    started = []

    def send(src, dst, send_sem, recv_sem, device):
        copy = pltpu.make_async_remote_copy(
            src_ref=src, dst_ref=dst, send_sem=send_sem, recv_sem=recv_sem,
            device_id=device, device_id_type=MESH,
        )
        copy.start()
        started.append(copy)
        return copy

    def over_y(n, src, dst):
        return {
            p: send(src(y_peer(p)), dst, y_send.at[n, p], y_recv.at[n, p], at(y_peer(p) * NJ + j))
            for p in far_first(NY)
        }

    def over_j(n, src, dst):
        return {
            p: send(src(j_peer(p)), dst, j_send.at[n, p], j_recv.at[n, p], at(y * NJ + j_peer(p)))
            for p in far_first(NJ)
        }

    def over_z(n, src, dst):
        return {
            p: send(src(z_peer(p)), dst, z_send.at[n, p], z_recv.at[n, p], at(y * NJ + z_peer(p) * NC + c))
            for p in far_first(NZ)
        }

    def over_x(n, src, dst):
        return {
            p: send(src(x_peer(p)), dst, x_send.at[n, p], x_recv.at[n, p], at(s, x_peer(p)))
            for p in far_first(NX)
        }

    def span(ref, i, size):
        return ref.at[pl.ds(pl.multiple_of(i * size, size), size)]

    def arrived(copies):
        for copy in copies.values() if isinstance(copies, dict) else copies:
            copy.wait_recv()

    barrier = pltpu.get_barrier_semaphore()
    peers = [at(y_peer(p) * NJ + j) for p in range(1, NY)]
    peers += [at(y * NJ + j_peer(p)) for p in range(1, NJ)]
    peers += [at(s, x_peer(p)) for p in range(1, NX)]
    peers += [at(up), at(down)]
    for peer in peers:
        pl.semaphore_signal(barrier, inc=1, device_id=peer, device_id_type=MESH)
    loads = [
        pltpu.make_async_copy(src, dst, in_sems.at[i])
        for i, (src, dst) in enumerate((
            (cot_in, cot), (owners_in, owners), (feats, table.at[pl.ds(HALO, COARSE)]),
            (counts_in, counts), (rows_in, rows), (wt_in, wt),
        ))
    ]
    for load in loads:
        load.start()
    table[pl.ds(HALO + COARSE + HALO, TAB - COARSE - 2 * HALO), :] = jnp.zeros(
        (TAB - COARSE - 2 * HALO, CIN), BF16
    )

    def ones(mask):
        return jnp.where(mask, 1.0, 0.0).astype(BF16)

    square = (TAB, TAB)
    loads[0].wait()
    c1s[...] = nt(ones(iota(square, 0) == iota(square, 1)), cot[...]).reshape(NY, NJ, WIDE).astype(BF16)
    pl.semaphore_wait(barrier, len(peers))

    cot_first = over_y(0, lambda d: c1s.at[d], c1.at[y])
    halo_up = send(
        feats.at[pl.ds(COARSE - HALO, HALO)], table.at[pl.ds(0, HALO)],
        e_send.at[0], e_recv.at[0], at(up),
    )
    halo_down = send(
        feats.at[pl.ds(0, HALO)], table.at[pl.ds(HALO + COARSE, HALO)],
        e_send.at[1], e_recv.at[1], at(down),
    )
    c1[y] = c1s[y]
    for load in loads[1:]:
        load.wait()
    line = iota((TAB, SLOTS), 0)
    spread = ones(iota((COARSE, SLOTS), 0) == (iota((COARSE, SLOTS), 1) >> 3))
    many = jnp.broadcast_to(counts[...], (8, COARSE)).astype(F32).astype(BF16)
    valid = (iota((1, SLOTS), 1) & 7).astype(F32) < nn(many, spread)[0:1]
    for k in range(KVOL):
        onehot[pl.ds(k * TAB, TAB), :] = ones(line == rows[k])
    to_j = ones(iota(square, 1) == (iota(square, 0) & (NY - 1)) * NJ + (iota(square, 0) >> 3))
    to_y = ones(iota(square, 1) == (iota(square, 0) & (NJ - 1)) * NY + (iota(square, 0) >> 4))

    arrived(cot_first)
    c2s[...] = nn(to_j, c1[...].reshape(NS, WIDE)).reshape(NJ, NY, WIDE).astype(BF16)
    cot_second = over_j(0, lambda d: c2s.at[d], c2.at[j])
    c2[j] = c2s[j]

    named = (line & (NY - 1)) * NJ + (line >> 3) == owners[...]
    earlier = ones(iota((SLOTS, SLOTS), 0) < iota((SLOTS, SLOTS), 1))
    before = nn(ones(named), earlier)
    for r in range(CAP):
        place[pl.ds(r * TAB, TAB), :] = ones(named & (before == r))

    arrived([halo_up, halo_down])

    @pl.when(s == 0)
    def _():
        table[pl.ds(0, HALO), :] = jnp.zeros((HALO, CIN), BF16)

    @pl.when(s == NS - 1)
    def _():
        table[pl.ds(HALO + COARSE, HALO), :] = jnp.zeros((HALO, CIN), BF16)

    features = table[...]
    turned = nt(ones(iota(square, 0) == iota(square, 1)), features).astype(BF16)
    for k in range(KVOL):
        here = pl.ds(k * TAB, TAB)
        found[here, :] = nn(turned, onehot[here, :]).astype(BF16)
    found[pl.ds(KVOL * TAB, TAB), :] = jnp.zeros((TAB, SLOTS), BF16)

    arrived(cot_second)
    turned = c2[...].astype(F32).reshape(NS, WIDE).T.astype(BF16)
    turned = jnp.concatenate([turned[r * COUT:(r + 1) * COUT] for r in range(CAP)], axis=1)
    slot_grad = jnp.where(valid, nn(turned, place[...]), 0.0).astype(BF16)
    def half(d):
        rows_of = pl.ds(pl.multiple_of(d * (KHALF * TAB), 16), KHALF * TAB)
        value = nt(slot_grad, found[rows_of, :])
        each = [value[:, k * TAB:(k + 1) * TAB] for k in range(KHALF)]
        core_a[d] = jnp.concatenate(each[:ROWS_A // COUT], axis=0).reshape(NX, NZ * PART, CIN)
        core_b[d] = jnp.concatenate(each[ROWS_A // COUT:], axis=0).reshape(NZ, PARTS_B * PART, CIN)

    order = (2, 1, 3, 0)
    half(1 - c)
    reduce_core_a = [
        send(core_a.at[1 - c, x_peer(p)], from_core_a.at[x_peer(p)], p_send.at[0, p], p_recv.at[0, p], at(partner))
        for p in order
    ]
    reduce_core_b = send(core_b.at[1 - c], from_core_b, p_send.at[0, NX], p_recv.at[0, NX], at(partner))
    half(c)
    reduce_x_a = []
    for p, copy in zip(order, reduce_core_a):
        arrived([copy])
        d = x_peer(p)
        x_a[d] = core_a[c, d] + from_core_a[d]
        if p:
            reduce_x_a.append(send(x_a.at[d], from_x_a.at[x], x_send.at[0, p], x_recv.at[0, p], at(s, d)))
    arrived([reduce_core_b])
    y_b[...] = core_b[c] + from_core_b[...]
    reduce_y_b = over_y(3, lambda d: y_b.at[d], from_y_b.at[y])
    kernels = jnp.concatenate([wt[pl.ds(k * COUT, COUT), :] for k in range(KVOL)], axis=1)
    totals = nn(kernels, found[pl.ds(0, KVOL * TAB), :])
    slot_out = jnp.where(valid, totals, 0.0).astype(BF16)
    for r in range(CAP):
        f1s[:, :, pl.ds(r * COUT, COUT)] = (
            nt(place[pl.ds(r * TAB, TAB), :], slot_out).reshape(NJ, NY, COUT).astype(BF16)
        )
    fine_first = over_j(1, lambda d: f1s.at[d], f1.at[j])
    f1[j] = f1s[j]

    high, low = split(nt(slot_grad, onehot[...]))
    for k in range(KVOL):
        st[pl.ds(k * COUT, COUT), pl.ds(0, TAB)] = high[:, k * TAB:(k + 1) * TAB]
        st[pl.ds(k * COUT, COUT), pl.ds(TAB, TAB)] = low[:, k * TAB:(k + 1) * TAB]
    total = dot(st[...], wt[...], ((0,), (0,)))
    grad[...] = total[:TAB] + total[TAB:]
    rim_down = send(grad.at[pl.ds(0, HALO)], rim_high, e_send.at[2], e_recv.at[2], at(down))
    rim_up = send(
        grad.at[pl.ds(HALO + COARSE, HALO)], rim_low, e_send.at[3], e_recv.at[3], at(up)
    )
    x_b[NX - 1] = jnp.zeros((PART, CIN), F32)

    arrived(reduce_x_a)
    mine = x_a[x]
    for p in range(1, NX):
        mine = mine + from_x_a[x_peer(p)]
    z_a[...] = mine.reshape(NZ, PART, CIN)
    reduce_z_a = over_z(1, lambda d: z_a.at[d], from_z_a.at[z])

    arrived(reduce_y_b)
    mine = y_b[y]
    for p in range(1, NY):
        mine = mine + from_y_b[y_peer(p)]
    x_b[pl.ds(0, PARTS_B)] = mine.reshape(PARTS_B, PART, CIN)
    reduce_x_b = over_x(1, lambda d: x_b.at[d], from_x_b.at[x])

    arrived(fine_first)
    f2s[...] = (
        nn(to_y, f1[...].astype(F32).reshape(NS, WIDE).astype(BF16)).astype(BF16).reshape(NY, NJ, WIDE)
    )
    fine_second = over_y(1, lambda d: f2s.at[d], f2.at[y])
    f2[y] = f2s[y]

    arrived(reduce_z_a)
    mine = z_a[z]
    for p in range(1, NZ):
        mine = mine + from_z_a[z_peer(p)]
    y_a[...] = mine
    exchange_y_a = over_y(2, lambda d: y_a, from_y_a.at[y])
    from_y_a[y] = mine

    arrived(reduce_x_b)
    mine = x_b[x]
    for p in range(1, NX):
        mine = mine + from_x_b[x_peer(p)]
    z_b[...] = mine
    exchange_z_b = over_z(0, lambda d: z_b, from_z_b.at[z])
    from_z_b[z] = mine

    arrived([rim_down, rim_up])
    own = grad[pl.ds(HALO, COARSE), :]
    low = rim_low[...] * jnp.where(s == 0, 0.0, 1.0)
    high = rim_high[...] * jnp.where(s == NS - 1, 0.0, 1.0)
    coarse[pl.ds(0, HALO), :] = (own[:HALO] + low).astype(BF16)
    coarse[pl.ds(HALO, COARSE - 2 * HALO), :] = own[HALO:COARSE - HALO].astype(BF16)
    coarse[pl.ds(COARSE - HALO, HALO), :] = (own[COARSE - HALO:] + high).astype(BF16)

    arrived(exchange_y_a)
    done = from_y_a[0]
    for q in range(1, NY):
        done = done + from_y_a[q]
    done_a[...] = done
    gather_z_a = over_z(2, lambda d: done_a, span(all_z_a, z, PART))
    span(all_z_a, z, PART)[...] = done

    arrived(exchange_z_b)
    done = from_z_b[0]
    for q in range(1, NZ):
        done = done + from_z_b[q]
    done_b[...] = done
    gather_x_b = over_x(2, lambda d: done_b, span(all_x_b, x, PART))
    span(all_x_b, x, PART)[...] = done

    arrived(fine_second)
    fine[...] = f2[...].astype(F32).reshape(NS, WIDE).T.astype(BF16)

    arrived(gather_x_b)
    wide_a, wide_b = NZ * PART, PARTS_B * PART
    whole_b = all_x_b.at[pl.ds(0, wide_b)]
    gather_y_b = over_y(4, lambda d: whole_b, span(out_b.at[c], y, wide_b))
    gather_core = [send(whole_b, span(out_b.at[c], y, wide_b), p_send.at[1, NX], p_recv.at[1, NX], at(partner))]
    span(out_b.at[c], y, wide_b)[...] = whole_b[...]

    arrived(gather_z_a)
    gather_x_a = over_x(3, lambda d: all_z_a, span(out_a.at[c], x, wide_a))
    gather_core.append(send(all_z_a, span(out_a.at[c], x, wide_a), p_send.at[1, 0], p_recv.at[1, 0], at(partner)))
    span(out_a.at[c], x, wide_a)[...] = all_z_a[...]
    for p in (1, 7, 2, 6, 3, 5, 4):
        arrived([gather_y_b[p]])
        piece = span(out_b.at[c], (y + NY - p) % NY, wide_b)
        gather_core.append(send(piece, piece, p_send.at[1, NX + p], p_recv.at[1, NX + p], at(partner)))
    for p in (1, 3, 2):
        arrived([gather_x_a[p]])
        piece = span(out_a.at[c], (x + NX - p) % NX, wide_a)
        gather_core.append(send(piece, piece, p_send.at[1, p], p_recv.at[1, p], at(partner)))
    arrived(gather_core)
    for copy in started:
        copy.wait_send()


def finish_kernel(fine, coarse, part_a, part_b, fine_out, coarse_out, wgrad_out, sems):
    pairs = [(fine, fine_out), (coarse, coarse_out)]
    for c in range(NC):
        rest = min(ROWS_B, ROWS - c * HALF - ROWS_A)
        pairs.append((part_a.at[c], wgrad_out.at[pl.ds(c * HALF, ROWS_A)]))
        pairs.append((part_b.at[c, pl.ds(0, rest)], wgrad_out.at[pl.ds(c * HALF + ROWS_A, rest)]))
    copies = [pltpu.make_async_copy(src, dst, sems.at[i]) for i, (src, dst) in enumerate(pairs)]
    for copy in copies:
        copy.start()
    for copy in copies:
        copy.wait()


def on_device(coarse_features, child_counts, neighbour_rows, fine_owners, weights, cotangent):
    sem = pltpu.SemaphoreType.DMA
    vmem = pl.BlockSpec(memory_space=pltpu.VMEM)
    hbm = pl.BlockSpec(memory_space=pltpu.HBM)
    fine, coarse, part_a, part_b = pl.pallas_call(
        kernel,
        out_shape=(
            jax.ShapeDtypeStruct((WIDE, NS), BF16),
            jax.ShapeDtypeStruct((COARSE, CIN), BF16),
            jax.ShapeDtypeStruct((NC, ROWS_A, CIN), F32),
            jax.ShapeDtypeStruct((NC, ROWS_B, CIN), F32),
        ),
        in_specs=[hbm] * 6,
        out_specs=(vmem,) * 4,
        scratch_shapes=[
            pltpu.VMEM((1, COARSE), jnp.int32),
            pltpu.VMEM((KVOL, 1, SLOTS), jnp.int32),
            pltpu.VMEM((1, SLOTS), jnp.int32),
            pltpu.VMEM((ROWS, CIN), BF16),
            pltpu.VMEM((WIDE, NS), BF16),
            pltpu.VMEM((TAB, CIN), BF16),
            pltpu.VMEM((KVOL * TAB, SLOTS), BF16),
            pltpu.VMEM((CAP * TAB, SLOTS), BF16),
            pltpu.VMEM((NC * KHALF * TAB, SLOTS), BF16),
            pltpu.VMEM((ROWS, 2 * TAB), BF16),
            pltpu.VMEM((NY, NJ, WIDE), BF16),
            pltpu.VMEM((NY, NJ, WIDE), BF16),
            pltpu.VMEM((NJ, NY, WIDE), BF16),
            pltpu.VMEM((NJ, NY, WIDE), BF16),
            pltpu.VMEM((NJ, NY, WIDE), BF16),
            pltpu.VMEM((NJ, NY, WIDE), BF16),
            pltpu.VMEM((NY, NJ, WIDE), BF16),
            pltpu.VMEM((NY, NJ, WIDE), BF16),
            pltpu.VMEM((TAB, CIN), F32),
            pltpu.VMEM((HALO, CIN), F32),
            pltpu.VMEM((HALO, CIN), F32),
            pltpu.VMEM((NC, NX, NZ * PART, CIN), F32),
            pltpu.VMEM((NX, NZ * PART, CIN), F32),
            pltpu.VMEM((NC, NZ, PARTS_B * PART, CIN), F32),
            pltpu.VMEM((NZ, PARTS_B * PART, CIN), F32),
            pltpu.VMEM((NX, NZ * PART, CIN), F32),
            pltpu.VMEM((NX, NZ * PART, CIN), F32),
            pltpu.VMEM((NZ, PART, CIN), F32),
            pltpu.VMEM((NZ, PART, CIN), F32),
            pltpu.VMEM((PART, CIN), F32),
            pltpu.VMEM((NY, PART, CIN), F32),
            pltpu.VMEM((PART, CIN), F32),
            pltpu.VMEM((NZ * PART, CIN), F32),
            pltpu.VMEM((NZ, PARTS_B * PART, CIN), F32),
            pltpu.VMEM((NZ, PARTS_B * PART, CIN), F32),
            pltpu.VMEM((NX, PART, CIN), F32),
            pltpu.VMEM((NX, PART, CIN), F32),
            pltpu.VMEM((PART, CIN), F32),
            pltpu.VMEM((NY, PART, CIN), F32),
            pltpu.VMEM((PART, CIN), F32),
            pltpu.VMEM((NX * PART, CIN), F32),
            sem((5, NY)), sem((5, NY)),
            sem((2, NJ)), sem((2, NJ)),
            sem((4,)), sem((4,)),
            sem((4, NZ)), sem((4, NZ)),
            sem((4, NX)), sem((4, NX)),
            sem((2, NX + NZ)), sem((2, NX + NZ)),
            sem((6,)),
        ],
        compiler_params=pltpu.CompilerParams(
            collective_id=0, has_side_effects=True, vmem_limit_bytes=48 * 1024 * 1024
        ),
        cost_estimate=pl.CostEstimate(flops=2_000_000_000, bytes_accessed=4_000_000, transcendentals=0),
    )(*(
        pltpu.with_memory_space_constraint(operand, pltpu.HBM)
        for operand in (
            coarse_features[0],
            child_counts,
            neighbour_rows.reshape(KVOL, 1, SLOTS),
            fine_owners.reshape(1, SLOTS),
            weights.transpose(0, 2, 1).reshape(ROWS, CIN),
            cotangent[0].transpose(1, 2, 0).reshape(WIDE, NS),
        )
    ))
    fine, coarse, wgrad = pl.pallas_call(
        finish_kernel,
        out_shape=(
            jax.ShapeDtypeStruct((WIDE, NS), BF16),
            jax.ShapeDtypeStruct((COARSE, CIN), BF16),
            jax.ShapeDtypeStruct((ROWS, CIN), F32),
        ),
        in_specs=[vmem] * 4,
        out_specs=(hbm,) * 3,
        scratch_shapes=[sem((6,))],
        compiler_params=pltpu.CompilerParams(vmem_limit_bytes=4 * 1024 * 1024),
    )(fine, coarse, part_a, part_b)
    return (
        fine.reshape(CAP, COUT, NS).transpose(2, 0, 1)[None],
        coarse[None],
        wgrad.reshape(KVOL, COUT, CIN).transpose(0, 2, 1),
    )


def solution(mesh):
    return jax.shard_map(
        on_device,
        mesh=mesh,
        in_specs=(
            P("scene", "space", None),
            P("scene", "space"),
            P("scene", None, "space"),
            P("scene", "space", None),
            P(),
            P("scene", "space", None, None),
        ),
        out_specs=(P("scene", "space", None, None), P("scene", "space", None), P()),
        check_vma=False,
    )
```

```python
import jax
import jax.numpy as jnp
from jax import lax
from jax.experimental import pallas as pl
from jax.experimental.pallas import tpu as pltpu
from jax.sharding import PartitionSpec as P

KVOL, CIN, COUT = 27, 128, 64
SLOTS, COARSE, HALO, CAP = 512, 64, 16, 6
NY, NZ, NC, NX = 8, 8, 2, 4
NJ = NZ * NC
NS = NY * NJ
TAB = 128
WIDE = CAP * COUT
ROWS = KVOL * COUT
KHALF = (KVOL + 1) // NC
HALF = KHALF * COUT
PART = 16
PARTS_B = 3
ROWS_A = NX * NZ * PART
ROWS_B = NZ * PARTS_B * PART
MESH = pl.DeviceIdType.MESH
F32, BF16 = jnp.float32, jnp.bfloat16


def dot(a, b, dims):
    return lax.dot_general(a, b, (dims, ((), ())), preferred_element_type=F32)


def nn(a, b):
    return dot(a, b, ((1,), (0,)))


def nt(a, b):
    return dot(a, b, ((1,), (1,)))


def split(value):
    high = value.astype(BF16)
    return high, (value - high.astype(F32)).astype(BF16)


def iota(shape, dim):
    return lax.broadcasted_iota(jnp.int32, shape, dim)


def far_first(n):
    return sorted(range(1, n), key=lambda p: -min(p, n - p))


def kernel(
    feats, counts_in, rows_in, owners_in, wt_in, cot_in,
    fine, coarse, out_a, out_b,
    counts, rows, owners, wt, cot,
    table, onehot, place, found, st,
    c1s, c1, c2s, c2, f1s, f1, f2s, f2,
    grad, rim_low, rim_high,
    core_a, from_core_a, core_b, from_core_b,
    x_a, from_x_a, z_a, from_z_a, y_a, from_y_a, done_a, all_z_a,
    y_b, from_y_b, x_b, from_x_b, z_b, from_z_b, done_b, all_x_b,
    y_send, y_recv, j_send, j_recv, e_send, e_recv,
    z_send, z_recv, x_send, x_recv, p_send, p_recv, in_sems,
):
    s, x = lax.axis_index("space"), lax.axis_index("scene")
    y, j = s // NJ, s % NJ
    z, c = j // NC, j % NC
    up, down = (s + 1) % NS, (s + NS - 1) % NS
    partner = y * NJ + z * NC + 1 - c

    def at(space, scene=None):
        return {"space": space, "scene": x if scene is None else scene}

    def y_peer(p):
        return (y + p) % NY

    def j_peer(p):
        return (j + p) % NJ

    def z_peer(p):
        return (z + p) % NZ

    def x_peer(p):
        return (x + p) % NX

    started = []

    def send(src, dst, send_sem, recv_sem, device):
        copy = pltpu.make_async_remote_copy(
            src_ref=src, dst_ref=dst, send_sem=send_sem, recv_sem=recv_sem,
            device_id=device, device_id_type=MESH,
        )
        copy.start()
        started.append(copy)
        return copy

    def over_y(n, src, dst):
        return {
            p: send(src(y_peer(p)), dst, y_send.at[n, p], y_recv.at[n, p], at(y_peer(p) * NJ + j))
            for p in far_first(NY)
        }

    def over_j(n, src, dst):
        return {
            p: send(src(j_peer(p)), dst, j_send.at[n, p], j_recv.at[n, p], at(y * NJ + j_peer(p)))
            for p in far_first(NJ)
        }

    def over_z(n, src, dst):
        return {
            p: send(src(z_peer(p)), dst, z_send.at[n, p], z_recv.at[n, p], at(y * NJ + z_peer(p) * NC + c))
            for p in far_first(NZ)
        }

    def over_x(n, src, dst):
        return {
            p: send(src(x_peer(p)), dst, x_send.at[n, p], x_recv.at[n, p], at(s, x_peer(p)))
            for p in far_first(NX)
        }

    def span(ref, i, size):
        return ref.at[pl.ds(pl.multiple_of(i * size, size), size)]

    def arrived(copies):
        for copy in copies.values() if isinstance(copies, dict) else copies:
            copy.wait_recv()

    barrier = pltpu.get_barrier_semaphore()
    peers = [at(y_peer(p) * NJ + j) for p in range(1, NY)]
    peers += [at(y * NJ + j_peer(p)) for p in range(1, NJ)]
    peers += [at(s, x_peer(p)) for p in range(1, NX)]
    peers += [at(up), at(down)]
    for peer in peers:
        pl.semaphore_signal(barrier, inc=1, device_id=peer, device_id_type=MESH)
    loads = [
        pltpu.make_async_copy(src, dst, in_sems.at[i])
        for i, (src, dst) in enumerate((
            (cot_in, cot), (owners_in, owners), (feats, table.at[pl.ds(HALO, COARSE)]),
            (counts_in, counts), (rows_in, rows), (wt_in, wt),
        ))
    ]
    for load in loads:
        load.start()
    table[pl.ds(HALO + COARSE + HALO, TAB - COARSE - 2 * HALO), :] = jnp.zeros(
        (TAB - COARSE - 2 * HALO, CIN), BF16
    )

    def ones(mask):
        return jnp.where(mask, 1.0, 0.0).astype(BF16)

    square = (TAB, TAB)
    loads[0].wait()
    c1s[...] = nt(ones(iota(square, 0) == iota(square, 1)), cot[...]).reshape(NY, NJ, WIDE).astype(BF16)
    pl.semaphore_wait(barrier, len(peers))

    cot_first = over_y(0, lambda d: c1s.at[d], c1.at[y])
    halo_up = send(
        feats.at[pl.ds(COARSE - HALO, HALO)], table.at[pl.ds(0, HALO)],
        e_send.at[0], e_recv.at[0], at(up),
    )
    halo_down = send(
        feats.at[pl.ds(0, HALO)], table.at[pl.ds(HALO + COARSE, HALO)],
        e_send.at[1], e_recv.at[1], at(down),
    )
    c1[y] = c1s[y]
    for load in loads[1:]:
        load.wait()
    line = iota((TAB, SLOTS), 0)
    spread = ones(iota((COARSE, SLOTS), 0) == (iota((COARSE, SLOTS), 1) >> 3))
    many = jnp.broadcast_to(counts[...], (8, COARSE)).astype(F32).astype(BF16)
    valid = (iota((1, SLOTS), 1) & 7).astype(F32) < nn(many, spread)[0:1]
    for k in range(KVOL):
        onehot[pl.ds(k * TAB, TAB), :] = ones(line == rows[k])
    to_j = ones(iota(square, 1) == (iota(square, 0) & (NY - 1)) * NJ + (iota(square, 0) >> 3))
    to_y = ones(iota(square, 1) == (iota(square, 0) & (NJ - 1)) * NY + (iota(square, 0) >> 4))

    arrived(cot_first)
    c2s[...] = nn(to_j, c1[...].reshape(NS, WIDE)).reshape(NJ, NY, WIDE).astype(BF16)
    cot_second = over_j(0, lambda d: c2s.at[d], c2.at[j])
    c2[j] = c2s[j]

    named = (line & (NY - 1)) * NJ + (line >> 3) == owners[...]
    earlier = ones(iota((SLOTS, SLOTS), 0) < iota((SLOTS, SLOTS), 1))
    before = nn(ones(named), earlier)
    for r in range(CAP):
        place[pl.ds(r * TAB, TAB), :] = ones(named & (before == r))

    arrived([halo_up, halo_down])

    @pl.when(s == 0)
    def _():
        table[pl.ds(0, HALO), :] = jnp.zeros((HALO, CIN), BF16)

    @pl.when(s == NS - 1)
    def _():
        table[pl.ds(HALO + COARSE, HALO), :] = jnp.zeros((HALO, CIN), BF16)

    features = table[...]
    turned = nt(ones(iota(square, 0) == iota(square, 1)), features).astype(BF16)
    for k in range(KVOL):
        here = pl.ds(k * TAB, TAB)
        found[here, :] = nn(turned, onehot[here, :]).astype(BF16)
    found[pl.ds(KVOL * TAB, TAB), :] = jnp.zeros((TAB, SLOTS), BF16)

    arrived(cot_second)
    turned = c2[...].astype(F32).reshape(NS, WIDE).T.astype(BF16)
    turned = jnp.concatenate([turned[r * COUT:(r + 1) * COUT] for r in range(CAP)], axis=1)
    slot_grad = jnp.where(valid, nn(turned, place[...]), 0.0).astype(BF16)
    def half(d):
        rows_of = pl.ds(pl.multiple_of(d * (KHALF * TAB), 16), KHALF * TAB)
        value = nt(slot_grad, found[rows_of, :])
        each = [value[:, k * TAB:(k + 1) * TAB] for k in range(KHALF)]
        core_a[d] = jnp.concatenate(each[:ROWS_A // COUT], axis=0).reshape(NX, NZ * PART, CIN)
        core_b[d] = jnp.concatenate(each[ROWS_A // COUT:], axis=0).reshape(NZ, PARTS_B * PART, CIN)

    order = (2, 1, 3, 0)
    half(1 - c)
    reduce_core_b = send(core_b.at[1 - c], from_core_b, p_send.at[0, NX], p_recv.at[0, NX], at(partner))
    reduce_core_a = [
        send(core_a.at[1 - c, x_peer(p)], from_core_a.at[x_peer(p)], p_send.at[0, p], p_recv.at[0, p], at(partner))
        for p in order
    ]
    half(c)
    arrived([reduce_core_b])
    y_b[...] = core_b[c] + from_core_b[...]
    reduce_y_b = over_y(3, lambda d: y_b.at[d], from_y_b.at[y])
    reduce_x_a = []
    for p, copy in zip(order, reduce_core_a):
        arrived([copy])
        d = x_peer(p)
        x_a[d] = core_a[c, d] + from_core_a[d]
        if p:
            reduce_x_a.append(send(x_a.at[d], from_x_a.at[x], x_send.at[0, p], x_recv.at[0, p], at(s, d)))
    kernels = jnp.concatenate([wt[pl.ds(k * COUT, COUT), :] for k in range(KVOL)], axis=1)
    totals = nn(kernels, found[pl.ds(0, KVOL * TAB), :])
    slot_out = jnp.where(valid, totals, 0.0).astype(BF16)
    for r in range(CAP):
        f1s[:, :, pl.ds(r * COUT, COUT)] = (
            nt(place[pl.ds(r * TAB, TAB), :], slot_out).reshape(NJ, NY, COUT).astype(BF16)
        )
    fine_first = over_j(1, lambda d: f1s.at[d], f1.at[j])
    f1[j] = f1s[j]

    high, low = split(nt(slot_grad, onehot[...]))
    for k in range(KVOL):
        st[pl.ds(k * COUT, COUT), pl.ds(0, TAB)] = high[:, k * TAB:(k + 1) * TAB]
        st[pl.ds(k * COUT, COUT), pl.ds(TAB, TAB)] = low[:, k * TAB:(k + 1) * TAB]
    total = dot(st[...], wt[...], ((0,), (0,)))
    grad[...] = total[:TAB] + total[TAB:]
    rim_down = send(grad.at[pl.ds(0, HALO)], rim_high, e_send.at[2], e_recv.at[2], at(down))
    rim_up = send(
        grad.at[pl.ds(HALO + COARSE, HALO)], rim_low, e_send.at[3], e_recv.at[3], at(up)
    )
    x_b[NX - 1] = jnp.zeros((PART, CIN), F32)

    arrived(reduce_x_a)
    mine = x_a[x]
    for p in range(1, NX):
        mine = mine + from_x_a[x_peer(p)]
    z_a[...] = mine.reshape(NZ, PART, CIN)
    reduce_z_a = over_z(1, lambda d: z_a.at[d], from_z_a.at[z])

    arrived(reduce_y_b)
    mine = y_b[y]
    for p in range(1, NY):
        mine = mine + from_y_b[y_peer(p)]
    x_b[pl.ds(0, PARTS_B)] = mine.reshape(PARTS_B, PART, CIN)
    reduce_x_b = over_x(1, lambda d: x_b.at[d], from_x_b.at[x])

    arrived(fine_first)
    f2s[...] = (
        nn(to_y, f1[...].astype(F32).reshape(NS, WIDE).astype(BF16)).astype(BF16).reshape(NY, NJ, WIDE)
    )
    fine_second = over_y(1, lambda d: f2s.at[d], f2.at[y])
    f2[y] = f2s[y]

    arrived(reduce_z_a)
    mine = z_a[z]
    for p in range(1, NZ):
        mine = mine + from_z_a[z_peer(p)]
    y_a[...] = mine
    exchange_y_a = over_y(2, lambda d: y_a, from_y_a.at[y])
    from_y_a[y] = mine

    arrived(reduce_x_b)
    mine = x_b[x]
    for p in range(1, NX):
        mine = mine + from_x_b[x_peer(p)]
    z_b[...] = mine
    exchange_z_b = over_z(0, lambda d: z_b, from_z_b.at[z])
    from_z_b[z] = mine

    arrived([rim_down, rim_up])
    own = grad[pl.ds(HALO, COARSE), :]
    low = rim_low[...] * jnp.where(s == 0, 0.0, 1.0)
    high = rim_high[...] * jnp.where(s == NS - 1, 0.0, 1.0)
    coarse[pl.ds(0, HALO), :] = (own[:HALO] + low).astype(BF16)
    coarse[pl.ds(HALO, COARSE - 2 * HALO), :] = own[HALO:COARSE - HALO].astype(BF16)
    coarse[pl.ds(COARSE - HALO, HALO), :] = (own[COARSE - HALO:] + high).astype(BF16)

    arrived(exchange_y_a)
    done = from_y_a[0]
    for q in range(1, NY):
        done = done + from_y_a[q]
    done_a[...] = done
    gather_z_a = over_z(2, lambda d: done_a, span(all_z_a, z, PART))
    span(all_z_a, z, PART)[...] = done

    arrived(exchange_z_b)
    done = from_z_b[0]
    for q in range(1, NZ):
        done = done + from_z_b[q]
    done_b[...] = done
    gather_x_b = over_x(2, lambda d: done_b, span(all_x_b, x, PART))
    span(all_x_b, x, PART)[...] = done

    arrived(fine_second)
    fine[...] = f2[...].astype(F32).reshape(NS, WIDE).T.astype(BF16)

    arrived(gather_x_b)
    wide_a, wide_b = NZ * PART, PARTS_B * PART
    whole_b = all_x_b.at[pl.ds(0, wide_b)]
    gather_y_b = over_y(4, lambda d: whole_b, span(out_b.at[c], y, wide_b))
    gather_core = [send(whole_b, span(out_b.at[c], y, wide_b), p_send.at[1, NX], p_recv.at[1, NX], at(partner))]
    span(out_b.at[c], y, wide_b)[...] = whole_b[...]

    arrived(gather_z_a)
    gather_x_a = over_x(3, lambda d: all_z_a, span(out_a.at[c], x, wide_a))
    gather_core.append(send(all_z_a, span(out_a.at[c], x, wide_a), p_send.at[1, 0], p_recv.at[1, 0], at(partner)))
    span(out_a.at[c], x, wide_a)[...] = all_z_a[...]
    for p in (1, 7, 2, 6, 3, 5, 4):
        arrived([gather_y_b[p]])
        piece = span(out_b.at[c], (y + NY - p) % NY, wide_b)
        gather_core.append(send(piece, piece, p_send.at[1, NX + p], p_recv.at[1, NX + p], at(partner)))
    for p in (1, 3, 2):
        arrived([gather_x_a[p]])
        piece = span(out_a.at[c], (x + NX - p) % NX, wide_a)
        gather_core.append(send(piece, piece, p_send.at[1, p], p_recv.at[1, p], at(partner)))
    arrived(gather_core)
    for copy in started:
        copy.wait_send()


def finish_kernel(fine, coarse, part_a, part_b, fine_out, coarse_out, wgrad_out, sems):
    pairs = [(fine, fine_out), (coarse, coarse_out)]
    for c in range(NC):
        rest = min(ROWS_B, ROWS - c * HALF - ROWS_A)
        pairs.append((part_a.at[c], wgrad_out.at[pl.ds(c * HALF, ROWS_A)]))
        pairs.append((part_b.at[c, pl.ds(0, rest)], wgrad_out.at[pl.ds(c * HALF + ROWS_A, rest)]))
    copies = [pltpu.make_async_copy(src, dst, sems.at[i]) for i, (src, dst) in enumerate(pairs)]
    for copy in copies:
        copy.start()
    for copy in copies:
        copy.wait()


def on_device(coarse_features, child_counts, neighbour_rows, fine_owners, weights, cotangent):
    sem = pltpu.SemaphoreType.DMA
    vmem = pl.BlockSpec(memory_space=pltpu.VMEM)
    hbm = pl.BlockSpec(memory_space=pltpu.HBM)
    fine, coarse, part_a, part_b = pl.pallas_call(
        kernel,
        out_shape=(
            jax.ShapeDtypeStruct((WIDE, NS), BF16),
            jax.ShapeDtypeStruct((COARSE, CIN), BF16),
            jax.ShapeDtypeStruct((NC, ROWS_A, CIN), F32),
            jax.ShapeDtypeStruct((NC, ROWS_B, CIN), F32),
        ),
        in_specs=[hbm] * 6,
        out_specs=(vmem,) * 4,
        scratch_shapes=[
            pltpu.VMEM((1, COARSE), jnp.int32),
            pltpu.VMEM((KVOL, 1, SLOTS), jnp.int32),
            pltpu.VMEM((1, SLOTS), jnp.int32),
            pltpu.VMEM((ROWS, CIN), BF16),
            pltpu.VMEM((WIDE, NS), BF16),
            pltpu.VMEM((TAB, CIN), BF16),
            pltpu.VMEM((KVOL * TAB, SLOTS), BF16),
            pltpu.VMEM((CAP * TAB, SLOTS), BF16),
            pltpu.VMEM((NC * KHALF * TAB, SLOTS), BF16),
            pltpu.VMEM((ROWS, 2 * TAB), BF16),
            pltpu.VMEM((NY, NJ, WIDE), BF16),
            pltpu.VMEM((NY, NJ, WIDE), BF16),
            pltpu.VMEM((NJ, NY, WIDE), BF16),
            pltpu.VMEM((NJ, NY, WIDE), BF16),
            pltpu.VMEM((NJ, NY, WIDE), BF16),
            pltpu.VMEM((NJ, NY, WIDE), BF16),
            pltpu.VMEM((NY, NJ, WIDE), BF16),
            pltpu.VMEM((NY, NJ, WIDE), BF16),
            pltpu.VMEM((TAB, CIN), F32),
            pltpu.VMEM((HALO, CIN), F32),
            pltpu.VMEM((HALO, CIN), F32),
            pltpu.VMEM((NC, NX, NZ * PART, CIN), F32),
            pltpu.VMEM((NX, NZ * PART, CIN), F32),
            pltpu.VMEM((NC, NZ, PARTS_B * PART, CIN), F32),
            pltpu.VMEM((NZ, PARTS_B * PART, CIN), F32),
            pltpu.VMEM((NX, NZ * PART, CIN), F32),
            pltpu.VMEM((NX, NZ * PART, CIN), F32),
            pltpu.VMEM((NZ, PART, CIN), F32),
            pltpu.VMEM((NZ, PART, CIN), F32),
            pltpu.VMEM((PART, CIN), F32),
            pltpu.VMEM((NY, PART, CIN), F32),
            pltpu.VMEM((PART, CIN), F32),
            pltpu.VMEM((NZ * PART, CIN), F32),
            pltpu.VMEM((NZ, PARTS_B * PART, CIN), F32),
            pltpu.VMEM((NZ, PARTS_B * PART, CIN), F32),
            pltpu.VMEM((NX, PART, CIN), F32),
            pltpu.VMEM((NX, PART, CIN), F32),
            pltpu.VMEM((PART, CIN), F32),
            pltpu.VMEM((NY, PART, CIN), F32),
            pltpu.VMEM((PART, CIN), F32),
            pltpu.VMEM((NX * PART, CIN), F32),
            sem((5, NY)), sem((5, NY)),
            sem((2, NJ)), sem((2, NJ)),
            sem((4,)), sem((4,)),
            sem((4, NZ)), sem((4, NZ)),
            sem((4, NX)), sem((4, NX)),
            sem((2, NX + NZ)), sem((2, NX + NZ)),
            sem((6,)),
        ],
        compiler_params=pltpu.CompilerParams(
            collective_id=0, has_side_effects=True, vmem_limit_bytes=48 * 1024 * 1024
        ),
        cost_estimate=pl.CostEstimate(flops=2_000_000_000, bytes_accessed=4_000_000, transcendentals=0),
    )(*(
        pltpu.with_memory_space_constraint(operand, pltpu.HBM)
        for operand in (
            coarse_features[0],
            child_counts,
            neighbour_rows.reshape(KVOL, 1, SLOTS),
            fine_owners.reshape(1, SLOTS),
            weights.transpose(0, 2, 1).reshape(ROWS, CIN),
            cotangent[0].transpose(1, 2, 0).reshape(WIDE, NS),
        )
    ))
    fine, coarse, wgrad = pl.pallas_call(
        finish_kernel,
        out_shape=(
            jax.ShapeDtypeStruct((WIDE, NS), BF16),
            jax.ShapeDtypeStruct((COARSE, CIN), BF16),
            jax.ShapeDtypeStruct((ROWS, CIN), F32),
        ),
        in_specs=[vmem] * 4,
        out_specs=(hbm,) * 3,
        scratch_shapes=[sem((6,))],
        compiler_params=pltpu.CompilerParams(vmem_limit_bytes=4 * 1024 * 1024),
    )(fine, coarse, part_a, part_b)
    return (
        fine.reshape(CAP, COUT, NS).transpose(2, 0, 1)[None],
        coarse[None],
        wgrad.reshape(KVOL, COUT, CIN).transpose(0, 2, 1),
    )


def solution(mesh):
    return jax.shard_map(
        on_device,
        mesh=mesh,
        in_specs=(
            P("scene", "space", None),
            P("scene", "space"),
            P("scene", None, "space"),
            P("scene", "space", None),
            P(),
            P("scene", "space", None, None),
        ),
        out_specs=(P("scene", "space", None, None), P("scene", "space", None), P()),
        check_vma=False,
    )
```
